32 devices in a mesh: groups: 2 (over x), pool: 8 (over z, y), section: 2 (over core).
Axes of the slice: x: 2, y: 2, z: 4, core: 2. Of those that a mesh axis runs over, the one named last changes fastest.
Arguments:
- x_gate: bfloat16 [2, 16, 128, 16384], P('section', ('groups', 'pool')), parts along dimension 1, may hold values from -6 to 6
- dt_raw: bfloat16 [2, 16, 128, 8192], P('section', ('groups', 'pool')), parts along dimension 1, may hold values from -2 to 8
- state_maps: bfloat16 [2, 16, 128, 32], P('section', ('groups', 'pool')), parts along dimension 1, may hold values from -6 to 6
- a_log: float32 [2, 16, 8192], P('section'), may hold values from 0 to 2.77
- conv_weight: float32 [2, 4, 8192], P('section'), may hold values from -3 to 3
- dt_bias: float32 [2, 8192], P('section'), may hold values from -8.6 to -2.4
- d_skip: float32 [2, 8192], P('section'), may hold values from 0.1 to 1.9
- state_pool: float32 [2, 32, 16, 8192], P('section', ('groups', 'pool')), parts along dimension 1, may hold values from -6 to 6
- conv_pool: bfloat16 [2, 32, 3, 8192], P('section', ('groups', 'pool')), parts along dimension 1, may hold values from -6 to 6
- queries: bfloat16 [2, 16, 128, 2048], P('section', ('groups', 'pool')), parts along dimension 1, may hold values from -18 to 18
- suffix_kv: bfloat16 [2, 16, 128, 1024], P('section', ('groups', 'pool')), parts along dimension 1, may hold values from -6 to 6
- kv_pool: bfloat16 [2, 128, 64, 1024], P('section', ('groups', 'pool')), parts along dimension 1, may hold values from -10.5 to 10.5
- state_slot: int32 [2, 16], P('section', ('groups', 'pool')), parts along dimension 1, may hold values from 0 to 15, as said below
- kv_ids: int32 [2, 16, 8], P('section', ('groups', 'pool')), parts along dimension 1, may hold values from 0 to 63, as said below
- prefix_blocks: int32 [2, 16], P('section', ('groups', 'pool')), parts along dimension 1, may hold values from 1 to 8, as said below
Outputs:
- mamba_out: bfloat16 [2, 16, 128, 8192], P('section', ('groups', 'pool')), parts along dimension 1
- final_state: float32 [2, 16, 16, 8192], P('section', ('groups', 'pool')), parts along dimension 1
- attn_out: bfloat16 [2, 16, 128, 2048], P('section', ('groups', 'pool')), parts along dimension 1
The draws below stay inside these ranges and needn't reach their ends.
There are 2 independent parts, one for each index of `groups`. The reference program is written for one: setup_inputs(seed, part) draws one part's arguments, and reference() takes and returns one part's arrays. A program takes and returns all parts, laid end to end along the dimension named above; an argument that names none is the same for every part. Nothing has to cross between parts.
Inputs may be any that keep to these rules, and one draw needn't show every extreme that they name: `state_slot`: slot s of owner o is o * 2 + s; over the requests of a layer at most 1 distinct slots of one owner are named, and some owner has exactly 1. `kv_ids`: block b of owner o is o * 8 + b; a request's entries are distinct and all name cached blocks, those past its prefix too; over all entries of a layer at most 4 distinct blocks of one owner are named, and some owner has exactly 4. `prefix_blocks`: some request of each layer has 8.
All inputs are finite; a program needn't handle non-finite values.
Results may differ from the reference program's by a relative error of at most 0.0049.
Values may be sent and summed in bfloat16 or wider, within the bound.
A program may use at most 128 MiB of HBM per device.

```python
import math
import jax
import jax.numpy as jnp
from jax import lax

DI = 8192
NS = 16
KW = 4
HD = 128
HQ = 16
HK = 4
NEW_TOKENS = 128
BLK = 64
MAXB = 8
SSLOTS_DEV = 2
KSLOTS_DEV = 8
KREF = 4
LAYER_COUNT = 2
REQUEST_COUNT = 8
SSLOTS = 16
KSLOTS = 64
KVW = 1024
N_POOL = 8


def prefix_plan(key):
    trial_key, label_key, length_key, longest_key, state_key, block_key = jax.random.split(key, 6)
    trials = jax.random.randint(trial_key, (3, LAYER_COUNT, REQUEST_COUNT), 0, N_POOL)
    lowest = jnp.min(trials, axis=0)
    relabel = jax.random.permutation(label_key, N_POOL).astype(jnp.int32)
    owners = relabel[lowest]
    live_state = jax.random.randint(state_key, (LAYER_COUNT, N_POOL), 0, SSLOTS_DEV)
    row_keys = jax.random.split(block_key, LAYER_COUNT * N_POOL)

    def live_row(row_key):
        return jax.random.permutation(row_key, KSLOTS_DEV)[:KREF]
    live_blocks = jax.vmap(live_row)(row_keys).reshape(LAYER_COUNT, N_POOL, KREF).astype(jnp.int32)
    layer_ids = jnp.arange(LAYER_COUNT)[:, None]
    slot_ids = owners * SSLOTS_DEV + live_state[layer_ids, owners]
    positions = jnp.arange(MAXB)
    block_owner = (owners[:, :, None] + positions[None, None, :] // KREF) % N_POOL
    block_slot = live_blocks[layer_ids[:, :, None], block_owner, (positions % KREF)[None, None, :]]
    block_ids = block_owner * KSLOTS_DEV + block_slot
    lengths = jax.random.randint(length_key, (LAYER_COUNT, REQUEST_COUNT), 1, MAXB + 1)
    longest = jax.random.randint(longest_key, (LAYER_COUNT, 1), 0, REQUEST_COUNT)
    lengths = jnp.where(jnp.arange(REQUEST_COUNT)[None, :] == longest, MAXB, lengths)
    return (slot_ids.astype(jnp.int32), block_ids.astype(jnp.int32), lengths.astype(jnp.int32))


def draw_state_slot(key, part):
    return prefix_plan(key)[0]


def draw_kv_ids(key, part):
    return prefix_plan(key)[1]


def draw_prefix_blocks(key, part):
    return prefix_plan(key)[2]


def draw_queries(key, part):
    key = jax.random.fold_in(key, 21)
    dims_all = (LAYER_COUNT, REQUEST_COUNT, NEW_TOKENS, HQ * HD)
    value_rows = jnp.clip(jax.random.normal(key, dims_all, jnp.float32), -6.0, 6.0)
    return value_rows.astype(jnp.bfloat16)


def draw_kv_pool(key, part):
    key = jax.random.fold_in(key, 23)
    dims_all = (LAYER_COUNT, KSLOTS, BLK, KVW)
    value_rows = jnp.clip(jax.random.normal(key, dims_all, jnp.float32), -6.0, 6.0)
    return value_rows.astype(jnp.bfloat16)


def draw_dt_bias(key, part):
    key = jax.random.fold_in(key, 31)
    lower = jnp.log(0.0003)
    upper = jnp.log(0.08)
    step_rate = jnp.exp(jax.random.uniform(key, (LAYER_COUNT, DI), jnp.float32, lower, upper))
    return jnp.log(jnp.expm1(step_rate))


def draw_dt_raw(key, part):
    key = jax.random.fold_in(key, 41)
    random_base_key, request_group_key = jax.random.split(key)
    dims_all = (LAYER_COUNT, REQUEST_COUNT, NEW_TOKENS, DI)
    value_rows = jnp.clip(0.5 * jax.random.normal(random_base_key, dims_all, jnp.float32), -2.0, 2.0)
    group_start_row = jax.random.randint(request_group_key, (LAYER_COUNT, REQUEST_COUNT, 1, 3), 0, NEW_TOKENS)
    request_groups = jnp.any(jnp.arange(NEW_TOKENS)[None, None, :, None] == group_start_row, axis=-1)
    value_rows = value_rows + 6.0 * request_groups[..., None].astype(jnp.float32)
    return value_rows.astype(jnp.bfloat16)


def block_levels(rng, shape, shards, least, largest):
    def one(position, shards_of):
        draws = jax.random.uniform(jax.random.fold_in(jax.random.fold_in(rng, 6), position), (shards_of,), jnp.float32, least / len(shards), largest / len(shards))
        return jnp.repeat(jnp.exp(draws), shape[position] // shards_of).reshape((-1,) + (1,) * (len(shape) - position - 1))

    loudness = one(*shards[0])
    for cut in shards[1:]:
        loudness = loudness * one(*cut)
    return loudness


def bell_draw(stream_key, extent, width, limit, pieces=(), kind=jnp.bfloat16):
    loudness = block_levels(stream_key, extent, pieces, -0.22, 0.18) if pieces else 1.0
    values = jax.random.normal(stream_key, extent, jnp.float32) * width * loudness
    return jnp.minimum(jnp.maximum(values, -limit), limit).astype(kind)


def setup_inputs(seed: int = 0, part: int = 0) -> dict:
    key_of = jax.random.split(jax.random.key(seed), 16)
    own_keys = jax.random.split(jax.random.fold_in(key_of[15], part), 16)
    return {
        "x_gate": bell_draw(own_keys[0], (LAYER_COUNT, REQUEST_COUNT, NEW_TOKENS, 2 * DI), 1.0, 6.0, ((0, 2), (1, 8))),
        "dt_raw": draw_dt_raw(jax.random.fold_in(jax.random.fold_in(key_of[15], part), 71), part),
        "state_maps": bell_draw(own_keys[2], (LAYER_COUNT, REQUEST_COUNT, NEW_TOKENS, 2 * NS), 1.0, 6.0, ((0, 2), (1, 8))),
        "a_log": jnp.clip(2.77 * jax.random.uniform(key_of[3], (LAYER_COUNT, NS, DI), jnp.float32) ** block_levels(key_of[3], (LAYER_COUNT, NS, DI), ((0, 2),), -0.2, 0.2), 0.0, 2.77),
        "conv_weight": bell_draw(key_of[4], (LAYER_COUNT, KW, DI), KW ** -0.5, 3.0, ((0, 2),), jnp.float32),
        "dt_bias": draw_dt_bias(jax.random.fold_in(key_of[15], 71), part),
        "d_skip": jnp.clip(1.0 + 0.18 * jax.random.normal(key_of[6], (LAYER_COUNT, DI), jnp.float32), 0.1, 1.9),
        "state_pool": bell_draw(own_keys[7], (LAYER_COUNT, SSLOTS, NS, DI), 1.0, 6.0, ((0, 2), (1, 8)), jnp.float32),
        "conv_pool": bell_draw(own_keys[8], (LAYER_COUNT, SSLOTS, KW - 1, DI), 1.0, 6.0, ((0, 2), (1, 8))),
        "queries": draw_queries(jax.random.fold_in(jax.random.fold_in(key_of[15], part), 71), part),
        "suffix_kv": bell_draw(own_keys[10], (LAYER_COUNT, REQUEST_COUNT, NEW_TOKENS, KVW), 1.0, 6.0, ((0, 2), (1, 8))),
        "kv_pool": draw_kv_pool(jax.random.fold_in(jax.random.fold_in(key_of[15], part), 71), part),
        "state_slot": draw_state_slot(jax.random.fold_in(jax.random.fold_in(key_of[15], part), 71), part),
        "kv_ids": draw_kv_ids(jax.random.fold_in(jax.random.fold_in(key_of[15], part), 71), part),
        "prefix_blocks": draw_prefix_blocks(jax.random.fold_in(jax.random.fold_in(key_of[15], part), 71), part),
    }


def mixer(x_gate, dt_raw, state_maps, start_state, conv_state, a_log, conv_weight, dt_bias, d_skip):
    inputs_part = x_gate[:, :DI].astype(jnp.float32)
    gate_part = x_gate[:, DI:].astype(jnp.float32)
    padded = jnp.concatenate([conv_state.astype(jnp.float32), inputs_part], axis=0)
    convolved = conv_weight[0][None, :] * padded[0:NEW_TOKENS]
    for offset in range(1, KW):
        convolved = convolved + conv_weight[offset][None, :] * padded[offset:offset + NEW_TOKENS]
    signal = jax.nn.silu(convolved)
    step_rate = jax.nn.softplus(dt_raw.astype(jnp.float32) + dt_bias[None, :])
    decay_coef = -jnp.exp(a_log)
    b_part = state_maps[:, :NS].astype(jnp.float32)
    c_part = state_maps[:, NS:].astype(jnp.float32)

    def advance(ssm_state, inputs):
        rate_now, signal_now, b_now, c_now = inputs
        ssm_state = jnp.exp(rate_now[None, :] * decay_coef) * ssm_state + (rate_now * signal_now)[None, :] * b_now[:, None]
        return (ssm_state, lax.optimization_barrier(jnp.sum(c_now[:, None] * ssm_state, axis=0)))
    last_state, outputs = lax.scan(advance, start_state, (step_rate, signal, b_part, c_part))
    result = ((outputs + d_skip[None, :] * signal) * jax.nn.silu(gate_part)).astype(jnp.bfloat16)
    return (result, last_state)

def attend(queries, suffix_kv, blocks, used_blocks):
    prefix_rows = MAXB * BLK
    key_count = prefix_rows + NEW_TOKENS
    group_size = HQ // HK
    score_scale = 1.0 / math.sqrt(HD)
    keys_all = jnp.concatenate([blocks.reshape(prefix_rows, KVW), suffix_kv], axis=0)
    key_heads = keys_all[:, :HK * HD].reshape(key_count, HK, HD).astype(jnp.float32)
    value_heads = keys_all[:, HK * HD:].reshape(key_count, HK, HD).astype(jnp.float32)
    query_heads = queries.reshape(NEW_TOKENS, HK, group_size, HD).astype(jnp.float32)
    scores = jnp.einsum('tkgd,skd->kgts', query_heads, key_heads) * score_scale
    positions = jnp.arange(key_count, dtype=jnp.int32)[None, :]
    query_rows = jnp.arange(NEW_TOKENS, dtype=jnp.int32)[:, None]
    allowed = jnp.where(positions < prefix_rows, positions < used_blocks * BLK, positions - prefix_rows <= query_rows)
    scores = jnp.where(allowed[None, None], scores, -1e+30)
    row_max = lax.optimization_barrier(jnp.max(scores, axis=-1, keepdims=True))
    weights = jnp.exp(scores - row_max)
    probs = (weights / lax.optimization_barrier(jnp.sum(weights, axis=-1, keepdims=True))).astype(jnp.bfloat16)
    mixed = jnp.einsum('kgts,skd->tkgd', probs.astype(jnp.float32), value_heads)
    return mixed.reshape(NEW_TOKENS, HQ * HD).astype(jnp.bfloat16)

def reference(x_gate, dt_raw, state_maps, a_log, conv_weight, dt_bias, d_skip, state_pool, conv_pool, queries, suffix_kv, kv_pool, state_slot, kv_ids, prefix_blocks):
    mixer_layers = []
    state_layers = []
    attend_layers = []
    for layer_index in range(LAYER_COUNT):

        def request_step(request):
            state_row = state_slot[layer_index, request]
            mixed_out, last_state = mixer(x_gate[layer_index, request], dt_raw[layer_index, request], state_maps[layer_index, request], state_pool[layer_index, state_row], conv_pool[layer_index, state_row], a_log[layer_index], conv_weight[layer_index], dt_bias[layer_index], d_skip[layer_index])
            blocks = jnp.take(kv_pool[layer_index], kv_ids[layer_index, request], axis=0)
            attended = attend(queries[layer_index, request], suffix_kv[layer_index, request], blocks, prefix_blocks[layer_index, request])
            return (mixed_out, last_state, attended)
        mixed_out, last_state, attended = lax.map(request_step, jnp.arange(REQUEST_COUNT, dtype=jnp.int32))
        mixer_layers.append(mixed_out)
        state_layers.append(last_state)
        attend_layers.append(attended)
    return (jnp.stack(mixer_layers), jnp.stack(state_layers), jnp.stack(attend_layers))
```

```python
import functools
import math

import jax
import jax.numpy as jnp
from jax import lax
from jax.experimental import pallas as pl
from jax.experimental.pallas import tpu as pltpu
from jax.sharding import PartitionSpec as P

DI = 8192
NS = 16
KW = 4
HD = 128
HQ = 16
HK = 4
NEW_TOKENS = 128
BLK = 64
KVW = 1024
LANES = 128
LIVE = 4
PIECE = DI // 8
GROUPS = PIECE // LANES
CONV_ROWS = 32
ST_ROWS = GROUPS * NS + CONV_ROWS
LOG2E = math.log2(math.e)
MESH = pl.DeviceIdType.MESH
BF = jnp.bfloat16
F32 = jnp.float32


def fetch_kernel(
    n,
    ids_ref,
    state_ref,
    conv_ref,
    kv_ref,
    st_out,
    kv_out,
    ids_all,
    ids_s,
    table,
    table_s,
    st_send,
    st_hold,
    st_send2,
    kv_send,
    kv_hold,
    kv_send2,
    local_sem,
    send_sem,
    recv_sem,
):
    me = lax.axis_index("pool")
    slots_here = state_ref.shape[0]
    blocks_here = kv_ref.shape[0]
    maxb = kv_out.shape[1]

    barrier = pltpu.get_barrier_semaphore()
    for k in range(1, n):
        pl.semaphore_signal(
            barrier, inc=1, device_id={"pool": lax.rem(me + k, n)}, device_id_type=MESH
        )
    pl.semaphore_wait(barrier, n - 1)

    def push(kind, k, src, dst):
        copy = pltpu.make_async_remote_copy(
            src_ref=src,
            dst_ref=dst,
            send_sem=send_sem.at[kind, k],
            recv_sem=recv_sem.at[kind, k],
            device_id={"pool": lax.rem(me + k, n)},
            device_id_type=MESH,
        )
        copy.start()
        return copy

    def peer(k):
        return lax.rem(me + k, n)

    copies = [push(0, k, ids_ref, ids_all.at[me]) for k in range(1, n)]
    ids_all[me] = ids_ref[...]
    for copy in copies:
        copy.wait()

    lane = lax.broadcasted_iota(jnp.int32, (8, LANES), 1)
    hit = jnp.zeros((8, LANES), jnp.int32)
    for r in range(n):
        hit = jnp.maximum(hit, (ids_all[r, :maxb] == lane).astype(jnp.int32))
    named = jnp.broadcast_to(jnp.max(hit, axis=0, keepdims=True), (8, LANES))
    rank = jnp.zeros((8, LANES), jnp.int32)
    inner = lax.rem(lane, blocks_here)
    for d in range(1, blocks_here):
        rank = rank + jnp.where(inner >= d, pltpu.roll(named, d, axis=1), 0)
    table[0:8] = named
    table[8:16] = rank
    to_s = [
        pltpu.make_async_copy(ids_all, ids_s, local_sem.at[0]),
        pltpu.make_async_copy(table, table_s, local_sem.at[1]),
    ]
    for copy in to_s:
        copy.start()
    for copy in to_s:
        copy.wait()

    slot = jnp.int32(0)
    for r in range(n):
        rel = ids_s[r, maxb, 0] - me * slots_here
        slot = jnp.where((rel >= 0) & (rel < slots_here), rel, slot)
    live = [jnp.int32(0)] * LIVE
    for j in range(blocks_here):
        is_named = table_s[0, me * blocks_here + j]
        at = table_s[8, me * blocks_here + j]
        for k in range(LIVE):
            live[k] = jnp.where((is_named == 1) & (at == k), j, live[k])

    for p in range(n):
        for j in range(GROUPS):
            lo = (p * GROUPS + j) * LANES
            st_send[p, j * NS : (j + 1) * NS, :] = state_ref[slot, :, lo : lo + LANES].astype(BF)
        st_send[p, GROUPS * NS :, :] = conv_ref[slot, p]
    st_first = [push(1, k, st_send.at[peer(k)], st_hold.at[me]) for k in range(1, n)]
    st_hold[me] = st_send[me]
    for p in range(n):
        for k in range(LIVE):
            kv_send[p, k] = kv_ref[live[k], :, p * LANES : (p + 1) * LANES]
    kv_first = [push(2, k, kv_send.at[peer(k)], kv_hold.at[me]) for k in range(1, n)]
    kv_hold[me] = kv_send[me]

    for copy in st_first:
        copy.wait()
    st_second = []
    for k in range(1, n):
        owner = ids_s[peer(k), maxb, 0] // slots_here
        st_send2[k] = st_hold[owner]
        st_second.append(push(3, k, st_send2.at[k], st_out.at[me]))
    st_out[me] = st_hold[ids_s[me, maxb, 0] // slots_here]

    for copy in kv_first:
        copy.wait()
    kv_second = []
    for k in range(1, n):
        for i in range(maxb):
            block = ids_s[peer(k), i, 0]
            kv_send2[k, i] = kv_hold[block // blocks_here, table_s[8, block]]
        kv_second.append(push(4, k, kv_send2.at[k], kv_out.at[me]))
    for i in range(maxb):
        block = ids_s[me, i, 0]
        kv_out[me, i] = kv_hold[block // blocks_here, table_s[8, block]]
    for copy in st_second + kv_second:
        copy.wait()


def fetch(state_slot, kv_ids, state_pool, conv_pool, kv_pool):
    n = lax.axis_size("pool")
    maxb = kv_ids.shape[0]
    ids = jnp.concatenate(
        [
            jnp.broadcast_to(kv_ids[:, None], (maxb, LANES)),
            jnp.broadcast_to(state_slot, (8, LANES)),
        ],
        axis=0,
    )
    slots = conv_pool.shape[0]
    conv = conv_pool.reshape(slots, KW - 1, n, GROUPS, LANES).transpose(0, 2, 3, 1, 4)
    conv = jnp.pad(conv, ((0, 0), (0, 0), (0, 0), (0, 1), (0, 0)))
    conv = conv.reshape(slots, n, CONV_ROWS, LANES)
    vmem = pl.BlockSpec(memory_space=pltpu.VMEM)
    return pl.pallas_call(
        functools.partial(fetch_kernel, n),
        out_shape=(
            jax.ShapeDtypeStruct((n, ST_ROWS, LANES), BF),
            jax.ShapeDtypeStruct((n, maxb, BLK, LANES), BF),
        ),
        in_specs=[vmem] * 4,
        out_specs=(vmem, vmem),
        scratch_shapes=[
            pltpu.VMEM((n, maxb + 8, LANES), jnp.int32),
            pltpu.SMEM((n, maxb + 8, LANES), jnp.int32),
            pltpu.VMEM((16, LANES), jnp.int32),
            pltpu.SMEM((16, LANES), jnp.int32),
            pltpu.VMEM((n, ST_ROWS, LANES), BF),
            pltpu.VMEM((n, ST_ROWS, LANES), BF),
            pltpu.VMEM((n, ST_ROWS, LANES), BF),
            pltpu.VMEM((n, LIVE, BLK, LANES), BF),
            pltpu.VMEM((n, LIVE, BLK, LANES), BF),
            pltpu.VMEM((n, maxb, BLK, LANES), BF),
            pltpu.SemaphoreType.DMA((2,)),
            pltpu.SemaphoreType.DMA((5, n)),
            pltpu.SemaphoreType.DMA((5, n)),
        ],
        compiler_params=pltpu.CompilerParams(
            collective_id=0, has_side_effects=True, vmem_limit_bytes=24 * 2**20
        ),
    )(ids, state_pool, conv, kv_pool)


CHUNKS = 2


def mixer_kernel(
    x_ref,
    g_ref,
    dt_ref,
    maps_ref,
    a_ref,
    w_ref,
    bias_ref,
    skip_ref,
    st_ref,
    out_ref,
    last_ref,
    rate_s,
    drive_s,
    y_s,
    sig_s,
    a_s,
    h_s,
    u_s,
):
    tokens = NEW_TOKENS
    for q in range(CHUNKS):
        conv_rows = st_ref[q, GROUPS * NS :, :].astype(F32)
        for j in range(GROUPS):
            col = pl.ds((q * GROUPS + j) * LANES, LANES)
            u_s[5:8, :] = conv_rows[KW * j : KW * j + KW - 1]
            u_s[8:, :] = x_ref[:, col].astype(F32)
            acc = w_ref[0:1, col] * u_s[5 : 5 + tokens, :]
            for k in range(1, KW):
                acc = acc + w_ref[k : k + 1, col] * u_s[5 + k : 5 + k + tokens, :]
            signal = acc / (1.0 + jnp.exp(-acc))
            v = dt_ref[:, col].astype(F32) + bias_ref[:, col]
            rate = jnp.maximum(v, 0.0) + jnp.log1p(jnp.exp(-jnp.abs(v)))
            sig_s[:, col] = signal
            rate_s[q, pl.ds(j, tokens, stride=8), :] = rate
            drive_s[q, pl.ds(j, tokens, stride=8), :] = rate * signal
            a_s[q, pl.ds(j, NS, stride=8), :] = -LOG2E * jnp.exp(a_ref[:, col])
            h_s[q, pl.ds(j, NS, stride=8), :] = st_ref[q, j * NS : (j + 1) * NS, :].astype(F32)

    def step(t, state):
        rows = pl.ds(pl.multiple_of(t * 8, 8), 8)
        rate = [rate_s[q, rows, :] for q in range(CHUNKS)]
        drive = [drive_s[q, rows, :] for q in range(CHUNKS)]
        total = [None] * CHUNKS
        new = []
        for m in range(NS):
            b = maps_ref[t, m]
            c = maps_ref[t, NS + m]
            for q in range(CHUNKS):
                decay = jnp.exp2(rate[q] * a_s[q, m * 8 : (m + 1) * 8, :])
                h = decay * state[m * CHUNKS + q] + drive[q] * b
                new.append(h)
                total[q] = c * h if total[q] is None else total[q] + c * h
        for q in range(CHUNKS):
            y_s[q, rows, :] = total[q]
        return tuple(new)

    first = tuple(
        h_s[q, m * 8 : (m + 1) * 8, :] for m in range(NS) for q in range(CHUNKS)
    )
    last = lax.fori_loop(0, tokens, step, first, unroll=2)
    for m in range(NS):
        for q in range(CHUNKS):
            h_s[q, m * 8 : (m + 1) * 8, :] = last[m * CHUNKS + q]
    for q in range(CHUNKS):
        for j in range(GROUPS):
            col = pl.ds((q * GROUPS + j) * LANES, LANES)
            last_ref[:, col] = h_s[q, pl.ds(j, NS, stride=8), :]
            gate = g_ref[:, col].astype(F32)
            y = y_s[q, pl.ds(j, tokens, stride=8), :] + skip_ref[:, col] * sig_s[:, col]
            out_ref[:, col] = (y * (gate / (1.0 + jnp.exp(-gate)))).astype(BF)


def mixer(x_gate, dt_raw, state_maps, a_log, conv_weight, dt_bias, d_skip, st):
    width = CHUNKS * PIECE
    steps = DI // width
    t = NEW_TOKENS
    return pl.pallas_call(
        mixer_kernel,
        grid=(steps,),
        out_shape=(
            jax.ShapeDtypeStruct((t, DI), BF),
            jax.ShapeDtypeStruct((NS, DI), F32),
        ),
        in_specs=[
            pl.BlockSpec((t, width), lambda i: (0, i)),
            pl.BlockSpec((t, width), lambda i: (0, i + steps)),
            pl.BlockSpec((t, width), lambda i: (0, i)),
            pl.BlockSpec(memory_space=pltpu.SMEM),
            pl.BlockSpec((NS, width), lambda i: (0, i)),
            pl.BlockSpec((KW, width), lambda i: (0, i)),
            pl.BlockSpec((1, width), lambda i: (0, i)),
            pl.BlockSpec((1, width), lambda i: (0, i)),
            pl.BlockSpec((CHUNKS, ST_ROWS, LANES), lambda i: (i, 0, 0)),
        ],
        out_specs=(
            pl.BlockSpec((t, width), lambda i: (0, i)),
            pl.BlockSpec((NS, width), lambda i: (0, i)),
        ),
        scratch_shapes=[
            pltpu.VMEM((CHUNKS, t * 8, LANES), F32),
            pltpu.VMEM((CHUNKS, t * 8, LANES), F32),
            pltpu.VMEM((CHUNKS, t * 8, LANES), F32),
            pltpu.VMEM((t, width), F32),
            pltpu.VMEM((CHUNKS, NS * 8, LANES), F32),
            pltpu.VMEM((CHUNKS, NS * 8, LANES), F32),
            pltpu.VMEM((t + 8, LANES), F32),
        ],
        compiler_params=pltpu.CompilerParams(vmem_limit_bytes=32 * 2**20),
        cost_estimate=pl.CostEstimate(
            flops=8 * t * DI * NS, bytes_accessed=10 * t * DI, transcendentals=t * DI * NS
        ),
    )(
        x_gate,
        x_gate,
        dt_raw,
        state_maps.astype(F32),
        a_log,
        conv_weight,
        dt_bias[None],
        d_skip[None],
        st,
    )


def attend_kernel(used_ref, q_ref, new_ref, k_ref, v_ref, out_ref):
    group = HQ // HK
    rows = group * NEW_TOKENS
    prefix = k_ref.shape[1] * BLK
    scale = 1.0 / math.sqrt(HD)
    used = used_ref[0]
    dims = (((1,), (1,)), ((), ()))
    for g in range(HK):
        q = jnp.concatenate(
            [q_ref[:, (g * group + i) * HD : (g * group + i + 1) * HD] for i in range(group)], axis=0
        )
        old_k = k_ref[g].reshape(prefix, HD)
        old_v = v_ref[g].reshape(prefix, HD)
        new_k = new_ref[:, g * HD : (g + 1) * HD]
        new_v = new_ref[:, (HK + g) * HD : (HK + g + 1) * HD]
        s_old = lax.dot_general(q, old_k, dims, preferred_element_type=F32) * scale
        s_new = lax.dot_general(q, new_k, dims, preferred_element_type=F32) * scale
        at = lax.broadcasted_iota(jnp.int32, (rows, prefix), 1)
        s_old = jnp.where(at < used * BLK, s_old, -1e30)
        key = lax.broadcasted_iota(jnp.int32, (rows, NEW_TOKENS), 1)
        query = lax.broadcasted_iota(jnp.int32, (rows, NEW_TOKENS), 0) % NEW_TOKENS
        s_new = jnp.where(key <= query, s_new, -1e30)
        top = jnp.maximum(
            jnp.max(s_old, axis=1, keepdims=True), jnp.max(s_new, axis=1, keepdims=True)
        )
        w_old = jnp.exp(s_old - top)
        w_new = jnp.exp(s_new - top)
        norm = 1.0 / (
            jnp.sum(w_old, axis=1, keepdims=True) + jnp.sum(w_new, axis=1, keepdims=True)
        )
        mixed = jnp.dot((w_old * norm).astype(BF), old_v, preferred_element_type=F32)
        mixed = mixed + jnp.dot((w_new * norm).astype(BF), new_v, preferred_element_type=F32)
        for i in range(group):
            out_ref[:, (g * group + i) * HD : (g * group + i + 1) * HD] = mixed[
                i * NEW_TOKENS : (i + 1) * NEW_TOKENS
            ].astype(BF)


def attend(queries, suffix_kv, heads, used):
    maxb = heads.shape[1]
    return pl.pallas_call(
        attend_kernel,
        grid=(1,),
        out_shape=jax.ShapeDtypeStruct((NEW_TOKENS, HQ * HD), BF),
        in_specs=[
            pl.BlockSpec(memory_space=pltpu.SMEM),
            pl.BlockSpec((NEW_TOKENS, HQ * HD), lambda i: (0, 0)),
            pl.BlockSpec((NEW_TOKENS, KVW), lambda i: (0, 0)),
            pl.BlockSpec((HK, maxb, BLK, HD), lambda i: (0, 0, 0, 0)),
            pl.BlockSpec((HK, maxb, BLK, HD), lambda i: (1, 0, 0, 0)),
        ],
        out_specs=pl.BlockSpec((NEW_TOKENS, HQ * HD), lambda i: (0, 0)),
        compiler_params=pltpu.CompilerParams(vmem_limit_bytes=32 * 2**20),
    )(used, queries, suffix_kv, heads, heads)


def fetch_any(state_slot, kv_ids, state_pool, conv_pool, kv_pool):
    n = lax.axis_size("pool")
    maxb = kv_ids.shape[0]
    slots = lax.all_gather(state_slot, "pool", axis=0, tiled=True)
    ids = lax.all_gather(kv_ids, "pool", axis=0, tiled=True)

    def move(pool, wanted, count):
        width = pool.size // pool.shape[0] // n
        rows = pool.reshape(pool.shape[0], n, width)
        held = lax.all_to_all(rows, "pool", split_axis=1, concat_axis=0, tiled=True)
        send = held.reshape(-1, width)[wanted].reshape(n, count, 1, width)
        return lax.all_to_all(send, "pool", split_axis=0, concat_axis=2, tiled=True)

    state = move(state_pool, slots, 1).reshape(NS, DI).astype(BF)
    conv = move(conv_pool, slots, 1).reshape(KW - 1, DI)
    blocks = move(kv_pool, ids, maxb).reshape(maxb, BLK, KVW // LANES, LANES)
    state = state.reshape(NS, 8, GROUPS, LANES).transpose(1, 2, 0, 3)
    conv = conv.reshape(KW - 1, 8, GROUPS, LANES).transpose(1, 2, 0, 3)
    conv = jnp.pad(conv, ((0, 0), (0, 0), (0, 1), (0, 0)))
    st = jnp.concatenate(
        [state.reshape(8, GROUPS * NS, LANES), conv.reshape(8, CONV_ROWS, LANES)], axis=1
    )
    return st, blocks.transpose(2, 0, 1, 3)


def on_device(
    x_gate,
    dt_raw,
    state_maps,
    a_log,
    conv_weight,
    dt_bias,
    d_skip,
    state_pool,
    conv_pool,
    queries,
    suffix_kv,
    kv_pool,
    state_slot,
    kv_ids,
    prefix_blocks,
):
    get = fetch if lax.axis_size("pool") == 8 else fetch_any
    st, heads = get(state_slot[0], kv_ids[0, 0], state_pool[0], conv_pool[0], kv_pool[0])
    mixed_out, last_state = mixer(
        x_gate[0, 0],
        dt_raw[0, 0],
        state_maps[0, 0],
        a_log[0],
        conv_weight[0],
        dt_bias[0],
        d_skip[0],
        st,
    )
    attended = attend(queries[0, 0], suffix_kv[0, 0], heads, prefix_blocks[0])
    return (mixed_out[None, None], last_state[None, None], attended[None, None])


def solution(mesh):
    placed = (
        P("section", ("groups", "pool"), None, None),
        P("section", ("groups", "pool"), None, None),
        P("section", ("groups", "pool"), None, None),
        P("section", None, None),
        P("section", None, None),
        P("section", None),
        P("section", None),
        P("section", ("groups", "pool"), None, None),
        P("section", ("groups", "pool"), None, None),
        P("section", ("groups", "pool"), None, None),
        P("section", ("groups", "pool"), None, None),
        P("section", ("groups", "pool"), None, None),
        P("section", ("groups", "pool")),
        P("section", ("groups", "pool"), None),
        P("section", ("groups", "pool")),
    )
    return jax.shard_map(
        on_device,
        mesh=mesh,
        in_specs=placed,
        out_specs=(
            P("section", ("groups", "pool"), None, None),
            P("section", ("groups", "pool"), None, None),
            P("section", ("groups", "pool"), None, None),
        ),
        check_vma=False,
    )
```

```python
import functools
import math

import jax
import jax.numpy as jnp
from jax import lax
from jax.experimental import pallas as pl
from jax.experimental.pallas import tpu as pltpu
from jax.sharding import PartitionSpec as P

DI = 8192
NS = 16
KW = 4
HD = 128
HQ = 16
HK = 4
NEW_TOKENS = 128
BLK = 64
KVW = 1024
LANES = 128
LIVE = 4
PIECE = DI // 8
GROUPS = PIECE // LANES
CONV_ROWS = 32
ST_ROWS = GROUPS * NS + CONV_ROWS
LOG2E = math.log2(math.e)
MESH = pl.DeviceIdType.MESH
BF = jnp.bfloat16
F32 = jnp.float32


CHUNKS = 2


def mix(i, maps_ref, a_ref, w_ref, skip_ref, x_ref, st_ref, out_ref, last_ref,
        rate_s, gate_s, drive_s, y_s, sig_s, a_s, h_s, u_s):
    tokens = NEW_TOKENS
    width = CHUNKS * PIECE

    def columns(q, j):
        return pl.ds(pl.multiple_of(i * width + (q * GROUPS + j) * LANES, LANES), LANES)

    for q in range(CHUNKS):
        p = i * CHUNKS + q
        conv_rows = st_ref[p, GROUPS * NS :, :].astype(F32)
        for j in range(GROUPS):
            col = columns(q, j)
            here = (q * GROUPS + j) * LANES
            u_s[5:8, :] = conv_rows[KW * j : KW * j + KW - 1]
            u_s[8:, :] = x_ref[:, col].astype(F32)
            acc = w_ref[0:1, col] * u_s[5 : 5 + tokens, :]
            for k in range(1, KW):
                acc = acc + w_ref[k : k + 1, col] * u_s[5 + k : 5 + k + tokens, :]
            signal = acc / (1.0 + jnp.exp(-acc))
            sig_s[:, here : here + LANES] = signal
            rate = rate_s[p, pl.ds(j, tokens, stride=8), :]
            drive_s[q, pl.ds(j, tokens, stride=8), :] = rate * signal
            a_s[pl.ds(q * 8 + j, NS, stride=8 * CHUNKS), :] = -LOG2E * jnp.exp(a_ref[:, col])
            h_s[pl.ds(q * 8 + j, NS, stride=8 * CHUNKS), :] = st_ref[
                p, j * NS : (j + 1) * NS, :
            ].astype(F32)

    tall = 8 * CHUNKS

    def step(t, state):
        rows = pl.ds(pl.multiple_of(t * 8, 8), 8)
        rate = jnp.concatenate([rate_s[i * CHUNKS + q, rows, :] for q in range(CHUNKS)], axis=0)
        drive = jnp.concatenate([drive_s[q, rows, :] for q in range(CHUNKS)], axis=0)
        total = None
        new = []
        for m in range(NS):
            b = maps_ref[t, m]
            c = maps_ref[t, NS + m]
            decay = jnp.exp2(rate * a_s[m * tall : (m + 1) * tall, :])
            h = decay * state[m] + drive * b
            new.append(h)
            total = c * h if total is None else total + c * h
        for q in range(CHUNKS):
            y_s[q, rows, :] = total[q * 8 : (q + 1) * 8]
        return tuple(new)

    first = tuple(h_s[m * tall : (m + 1) * tall, :] for m in range(NS))
    last = lax.fori_loop(0, tokens, step, first, unroll=2)
    for m in range(NS):
        h_s[m * tall : (m + 1) * tall, :] = last[m]
    for q in range(CHUNKS):
        for j in range(GROUPS):
            col = columns(q, j)
            here = (q * GROUPS + j) * LANES
            last_ref[:, col] = h_s[pl.ds(q * 8 + j, NS, stride=tall), :]
            y = y_s[q, pl.ds(j, tokens, stride=8), :] + skip_ref[:, col] * sig_s[:, here : here + LANES]
            out_ref[:, col] = (y * gate_s[:, col]).astype(BF)


def serve_kernel(
    n,
    ids_ref,
    maps_ref,
    conv_ref,
    a_ref,
    w_ref,
    bias_ref,
    skip_ref,
    state_hbm,
    kv_hbm,
    x_hbm,
    dt_hbm,
    out_ref,
    last_ref,
    kv_out,
    state_ref,
    kv_ref,
    x_ref,
    dt_ref,
    st_out,
    ids_all,
    ids_s,
    table,
    table_s,
    st_send,
    st_hold,
    st_send2,
    kv_send,
    kv_hold,
    kv_send2,
    rate_s,
    gate_s,
    drive_s,
    y_s,
    sig_s,
    a_s,
    h_s,
    u_s,
    local_sem,
    send_sem,
    recv_sem,
):
    me = lax.axis_index("pool")
    slots_here = state_ref.shape[0]
    blocks_here = kv_ref.shape[0]
    maxb = kv_out.shape[1]

    load_state, load_kv, load_dt, load_x = [
        pltpu.make_async_copy(src, dst, local_sem.at[2 + i])
        for i, (src, dst) in enumerate(
            ((state_hbm, state_ref), (kv_hbm, kv_ref), (dt_hbm, dt_ref), (x_hbm, x_ref))
        )
    ]
    for copy in (load_state, load_kv, load_dt, load_x):
        copy.start()

    barrier = pltpu.get_barrier_semaphore()
    for k in range(1, n):
        pl.semaphore_signal(
            barrier, inc=1, device_id={"pool": lax.rem(me + k, n)}, device_id_type=MESH
        )
    pl.semaphore_wait(barrier, n - 1)

    def push(kind, k, src, dst):
        copy = pltpu.make_async_remote_copy(
            src_ref=src,
            dst_ref=dst,
            send_sem=send_sem.at[kind, k],
            recv_sem=recv_sem.at[kind, k],
            device_id={"pool": lax.rem(me + k, n)},
            device_id_type=MESH,
        )
        copy.start()
        return copy

    def peer(k):
        return lax.rem(me + k, n)

    copies = [push(0, k, ids_ref, ids_all.at[me]) for k in range(1, n)]
    ids_all[me] = ids_ref[...]
    for copy in copies:
        copy.wait()

    lane = lax.broadcasted_iota(jnp.int32, (8, LANES), 1)
    hit = jnp.zeros((8, LANES), jnp.int32)
    for r in range(n):
        hit = jnp.maximum(hit, (ids_all[r, :maxb] == lane).astype(jnp.int32))
    named = jnp.broadcast_to(jnp.max(hit, axis=0, keepdims=True), (8, LANES))
    rank = jnp.zeros((8, LANES), jnp.int32)
    inner = lax.rem(lane, blocks_here)
    for d in range(1, blocks_here):
        rank = rank + jnp.where(inner >= d, pltpu.roll(named, d, axis=1), 0)
    table[0:8] = named
    table[8:16] = rank
    to_s = [
        pltpu.make_async_copy(ids_all, ids_s, local_sem.at[0]),
        pltpu.make_async_copy(table, table_s, local_sem.at[1]),
    ]
    for copy in to_s:
        copy.start()
    for copy in to_s:
        copy.wait()

    slot = jnp.int32(0)
    for r in range(n):
        rel = ids_s[r, maxb, 0] - me * slots_here
        slot = jnp.where((rel >= 0) & (rel < slots_here), rel, slot)
    live = [jnp.int32(0)] * LIVE
    for j in range(blocks_here):
        is_named = table_s[0, me * blocks_here + j]
        at = table_s[8, me * blocks_here + j]
        for k in range(LIVE):
            live[k] = jnp.where((is_named == 1) & (at == k), j, live[k])

    load_state.wait()
    for p in range(n):
        for j in range(GROUPS):
            lo = (p * GROUPS + j) * LANES
            st_send[p, j * NS : (j + 1) * NS, :] = state_ref[slot, :, lo : lo + LANES].astype(BF)
        st_send[p, GROUPS * NS :, :] = conv_ref[slot, p]
    st_first = [push(1, k, st_send.at[peer(k)], st_hold.at[me]) for k in range(1, n)]
    st_hold[me] = st_send[me]
    load_kv.wait()
    for p in range(n):
        for k in range(LIVE):
            kv_send[p, k] = kv_ref[live[k], :, p * LANES : (p + 1) * LANES]
    kv_first = [push(2, k, kv_send.at[peer(k)], kv_hold.at[me]) for k in range(1, n)]
    kv_hold[me] = kv_send[me]

    load_dt.wait()

    def rates(p, carry):
        for j in range(GROUPS):
            col = pl.ds(pl.multiple_of(p * PIECE + j * LANES, LANES), LANES)
            v = dt_ref[:, col].astype(F32) + bias_ref[:, col]
            rate = jnp.maximum(v, 0.0) + jnp.log1p(jnp.exp(-jnp.abs(v)))
            rate_s[p, pl.ds(j, NEW_TOKENS, stride=8), :] = rate
        return carry

    lax.fori_loop(0, DI // PIECE, rates, 0)

    for copy in st_first:
        copy.wait()
    st_second = []
    for k in range(1, n):
        owner = ids_s[peer(k), maxb, 0] // slots_here
        st_send2[k] = st_hold[owner]
        st_second.append(push(3, k, st_send2.at[k], st_out.at[me]))
    st_out[me] = st_hold[ids_s[me, maxb, 0] // slots_here]

    load_x.wait()

    def gates(p, carry):
        for j in range(GROUPS):
            col = pl.ds(pl.multiple_of(p * PIECE + j * LANES, LANES), LANES)
            far = pl.ds(pl.multiple_of(DI + p * PIECE + j * LANES, LANES), LANES)
            gate = x_ref[:, far].astype(F32)
            gate_s[:, col] = gate / (1.0 + jnp.exp(-gate))
        return carry

    lax.fori_loop(0, DI // PIECE, gates, 0)
    for copy in st_second:
        copy.wait()

    def run(i, carry):
        mix(i, maps_ref, a_ref, w_ref, skip_ref, x_ref, st_out, out_ref, last_ref,
            rate_s, gate_s, drive_s, y_s, sig_s, a_s, h_s, u_s)
        return carry

    run(0, 0)
    for copy in kv_first:
        copy.wait()
    kv_second = []
    for k in range(1, n):
        for i in range(maxb):
            block = ids_s[peer(k), i, 0]
            kv_send2[k, i] = kv_hold[block // blocks_here, table_s[8, block]]
        kv_second.append(push(4, k, kv_send2.at[k], kv_out.at[me]))
    for i in range(maxb):
        block = ids_s[me, i, 0]
        kv_out[me, i] = kv_hold[block // blocks_here, table_s[8, block]]
    lax.fori_loop(1, DI // (CHUNKS * PIECE), run, 0)
    for copy in kv_second:
        copy.wait()


def serve(
    state_slot, kv_ids, state_pool, conv_pool, kv_pool, x_gate, dt_raw, state_maps, a_log, conv_weight, dt_bias, d_skip
):
    n = lax.axis_size("pool")
    maxb = kv_ids.shape[0]
    ids = jnp.concatenate(
        [
            jnp.broadcast_to(kv_ids[:, None], (maxb, LANES)),
            jnp.broadcast_to(state_slot, (8, LANES)),
        ],
        axis=0,
    )
    slots = conv_pool.shape[0]
    conv = conv_pool.reshape(slots, KW - 1, n, GROUPS, LANES).transpose(0, 2, 3, 1, 4)
    conv = jnp.pad(conv, ((0, 0), (0, 0), (0, 0), (0, 1), (0, 0)))
    conv = conv.reshape(slots, n, CONV_ROWS, LANES)
    vmem = pl.BlockSpec(memory_space=pltpu.VMEM)
    return pl.pallas_call(
        functools.partial(serve_kernel, n),
        out_shape=(
            jax.ShapeDtypeStruct((NEW_TOKENS, DI), BF),
            jax.ShapeDtypeStruct((NS, DI), F32),
            jax.ShapeDtypeStruct((n, maxb, BLK, LANES), BF),
        ),
        in_specs=[vmem, pl.BlockSpec(memory_space=pltpu.SMEM)]
        + [vmem] * 5
        + [pl.BlockSpec(memory_space=pl.ANY)] * 4,
        out_specs=(vmem, vmem, vmem),
        scratch_shapes=[
            pltpu.VMEM(state_pool.shape, F32),
            pltpu.VMEM(kv_pool.shape, BF),
            pltpu.VMEM(x_gate.shape, BF),
            pltpu.VMEM(dt_raw.shape, BF),
            pltpu.VMEM((n, ST_ROWS, LANES), BF),
            pltpu.VMEM((n, maxb + 8, LANES), jnp.int32),
            pltpu.SMEM((n, maxb + 8, LANES), jnp.int32),
            pltpu.VMEM((16, LANES), jnp.int32),
            pltpu.SMEM((16, LANES), jnp.int32),
            pltpu.VMEM((n, ST_ROWS, LANES), BF),
            pltpu.VMEM((n, ST_ROWS, LANES), BF),
            pltpu.VMEM((n, ST_ROWS, LANES), BF),
            pltpu.VMEM((n, LIVE, BLK, LANES), BF),
            pltpu.VMEM((n, LIVE, BLK, LANES), BF),
            pltpu.VMEM((n, maxb, BLK, LANES), BF),
            pltpu.VMEM((DI // PIECE, NEW_TOKENS * 8, LANES), F32),
            pltpu.VMEM((NEW_TOKENS, DI), F32),
            pltpu.VMEM((CHUNKS, NEW_TOKENS * 8, LANES), F32),
            pltpu.VMEM((CHUNKS, NEW_TOKENS * 8, LANES), F32),
            pltpu.VMEM((NEW_TOKENS, CHUNKS * PIECE), F32),
            pltpu.VMEM((CHUNKS * NS * 8, LANES), F32),
            pltpu.VMEM((CHUNKS * NS * 8, LANES), F32),
            pltpu.VMEM((NEW_TOKENS + 8, LANES), F32),
            pltpu.SemaphoreType.DMA((6,)),
            pltpu.SemaphoreType.DMA((5, n)),
            pltpu.SemaphoreType.DMA((5, n)),
        ],
        compiler_params=pltpu.CompilerParams(
            collective_id=0, has_side_effects=True, vmem_limit_bytes=52 * 2**20
        ),
    )(
        ids,
        state_maps.astype(F32),
        conv,
        a_log,
        conv_weight,
        dt_bias[None],
        d_skip[None],
        state_pool,
        kv_pool,
        x_gate,
        dt_raw,
    )


def mixer_kernel(
    x_ref,
    g_ref,
    dt_ref,
    maps_ref,
    a_ref,
    w_ref,
    bias_ref,
    skip_ref,
    st_ref,
    out_ref,
    last_ref,
    rate_s,
    drive_s,
    y_s,
    sig_s,
    a_s,
    h_s,
    u_s,
):
    tokens = NEW_TOKENS
    for q in range(CHUNKS):
        conv_rows = st_ref[q, GROUPS * NS :, :].astype(F32)
        for j in range(GROUPS):
            col = pl.ds((q * GROUPS + j) * LANES, LANES)
            u_s[5:8, :] = conv_rows[KW * j : KW * j + KW - 1]
            u_s[8:, :] = x_ref[:, col].astype(F32)
            acc = w_ref[0:1, col] * u_s[5 : 5 + tokens, :]
            for k in range(1, KW):
                acc = acc + w_ref[k : k + 1, col] * u_s[5 + k : 5 + k + tokens, :]
            signal = acc / (1.0 + jnp.exp(-acc))
            v = dt_ref[:, col].astype(F32) + bias_ref[:, col]
            rate = jnp.maximum(v, 0.0) + jnp.log1p(jnp.exp(-jnp.abs(v)))
            sig_s[:, col] = signal
            rate_s[q, pl.ds(j, tokens, stride=8), :] = rate
            drive_s[q, pl.ds(j, tokens, stride=8), :] = rate * signal
            a_s[q, pl.ds(j, NS, stride=8), :] = -LOG2E * jnp.exp(a_ref[:, col])
            h_s[q, pl.ds(j, NS, stride=8), :] = st_ref[q, j * NS : (j + 1) * NS, :].astype(F32)

    def step(t, state):
        rows = pl.ds(pl.multiple_of(t * 8, 8), 8)
        rate = [rate_s[q, rows, :] for q in range(CHUNKS)]
        drive = [drive_s[q, rows, :] for q in range(CHUNKS)]
        total = [None] * CHUNKS
        new = []
        for m in range(NS):
            b = maps_ref[t, m]
            c = maps_ref[t, NS + m]
            for q in range(CHUNKS):
                decay = jnp.exp2(rate[q] * a_s[q, m * 8 : (m + 1) * 8, :])
                h = decay * state[m * CHUNKS + q] + drive[q] * b
                new.append(h)
                total[q] = c * h if total[q] is None else total[q] + c * h
        for q in range(CHUNKS):
            y_s[q, rows, :] = total[q]
        return tuple(new)

    first = tuple(
        h_s[q, m * 8 : (m + 1) * 8, :] for m in range(NS) for q in range(CHUNKS)
    )
    last = lax.fori_loop(0, tokens, step, first, unroll=2)
    for m in range(NS):
        for q in range(CHUNKS):
            h_s[q, m * 8 : (m + 1) * 8, :] = last[m * CHUNKS + q]
    for q in range(CHUNKS):
        for j in range(GROUPS):
            col = pl.ds((q * GROUPS + j) * LANES, LANES)
            last_ref[:, col] = h_s[q, pl.ds(j, NS, stride=8), :]
            gate = g_ref[:, col].astype(F32)
            y = y_s[q, pl.ds(j, tokens, stride=8), :] + skip_ref[:, col] * sig_s[:, col]
            out_ref[:, col] = (y * (gate / (1.0 + jnp.exp(-gate)))).astype(BF)


def mixer(x_gate, dt_raw, state_maps, a_log, conv_weight, dt_bias, d_skip, st):
    width = CHUNKS * PIECE
    steps = DI // width
    t = NEW_TOKENS
    return pl.pallas_call(
        mixer_kernel,
        grid=(steps,),
        out_shape=(
            jax.ShapeDtypeStruct((t, DI), BF),
            jax.ShapeDtypeStruct((NS, DI), F32),
        ),
        in_specs=[
            pl.BlockSpec((t, width), lambda i: (0, i)),
            pl.BlockSpec((t, width), lambda i: (0, i + steps)),
            pl.BlockSpec((t, width), lambda i: (0, i)),
            pl.BlockSpec(memory_space=pltpu.SMEM),
            pl.BlockSpec((NS, width), lambda i: (0, i)),
            pl.BlockSpec((KW, width), lambda i: (0, i)),
            pl.BlockSpec((1, width), lambda i: (0, i)),
            pl.BlockSpec((1, width), lambda i: (0, i)),
            pl.BlockSpec((CHUNKS, ST_ROWS, LANES), lambda i: (i, 0, 0)),
        ],
        out_specs=(
            pl.BlockSpec((t, width), lambda i: (0, i)),
            pl.BlockSpec((NS, width), lambda i: (0, i)),
        ),
        scratch_shapes=[
            pltpu.VMEM((CHUNKS, t * 8, LANES), F32),
            pltpu.VMEM((CHUNKS, t * 8, LANES), F32),
            pltpu.VMEM((CHUNKS, t * 8, LANES), F32),
            pltpu.VMEM((t, width), F32),
            pltpu.VMEM((CHUNKS, NS * 8, LANES), F32),
            pltpu.VMEM((CHUNKS, NS * 8, LANES), F32),
            pltpu.VMEM((t + 8, LANES), F32),
        ],
        compiler_params=pltpu.CompilerParams(vmem_limit_bytes=32 * 2**20),
        cost_estimate=pl.CostEstimate(
            flops=8 * t * DI * NS, bytes_accessed=10 * t * DI, transcendentals=t * DI * NS
        ),
    )(
        x_gate,
        x_gate,
        dt_raw,
        state_maps.astype(F32),
        a_log,
        conv_weight,
        dt_bias[None],
        d_skip[None],
        st,
    )


def attend_kernel(used_ref, q_ref, new_ref, k_ref, v_ref, out_ref):
    group = HQ // HK
    rows = group * NEW_TOKENS
    prefix = k_ref.shape[1] * BLK
    scale = 1.0 / math.sqrt(HD)
    used = used_ref[0]
    dims = (((1,), (1,)), ((), ()))
    for g in range(HK):
        q = jnp.concatenate(
            [q_ref[:, (g * group + i) * HD : (g * group + i + 1) * HD] for i in range(group)], axis=0
        )
        old_k = k_ref[g].reshape(prefix, HD)
        old_v = v_ref[g].reshape(prefix, HD)
        new_k = new_ref[:, g * HD : (g + 1) * HD]
        new_v = new_ref[:, (HK + g) * HD : (HK + g + 1) * HD]
        s_old = lax.dot_general(q, old_k, dims, preferred_element_type=F32) * scale
        s_new = lax.dot_general(q, new_k, dims, preferred_element_type=F32) * scale
        at = lax.broadcasted_iota(jnp.int32, (rows, prefix), 1)
        s_old = jnp.where(at < used * BLK, s_old, -1e30)
        key = lax.broadcasted_iota(jnp.int32, (rows, NEW_TOKENS), 1)
        query = lax.broadcasted_iota(jnp.int32, (rows, NEW_TOKENS), 0) % NEW_TOKENS
        s_new = jnp.where(key <= query, s_new, -1e30)
        top = jnp.maximum(
            jnp.max(s_old, axis=1, keepdims=True), jnp.max(s_new, axis=1, keepdims=True)
        )
        w_old = jnp.exp(s_old - top)
        w_new = jnp.exp(s_new - top)
        norm = 1.0 / (
            jnp.sum(w_old, axis=1, keepdims=True) + jnp.sum(w_new, axis=1, keepdims=True)
        )
        mixed = jnp.dot((w_old * norm).astype(BF), old_v, preferred_element_type=F32)
        mixed = mixed + jnp.dot((w_new * norm).astype(BF), new_v, preferred_element_type=F32)
        for i in range(group):
            out_ref[:, (g * group + i) * HD : (g * group + i + 1) * HD] = mixed[
                i * NEW_TOKENS : (i + 1) * NEW_TOKENS
            ].astype(BF)


def attend(queries, suffix_kv, heads, used):
    maxb = heads.shape[1]
    return pl.pallas_call(
        attend_kernel,
        grid=(1,),
        out_shape=jax.ShapeDtypeStruct((NEW_TOKENS, HQ * HD), BF),
        in_specs=[
            pl.BlockSpec(memory_space=pltpu.SMEM),
            pl.BlockSpec((NEW_TOKENS, HQ * HD), lambda i: (0, 0)),
            pl.BlockSpec((NEW_TOKENS, KVW), lambda i: (0, 0)),
            pl.BlockSpec((HK, maxb, BLK, HD), lambda i: (0, 0, 0, 0)),
            pl.BlockSpec((HK, maxb, BLK, HD), lambda i: (1, 0, 0, 0)),
        ],
        out_specs=pl.BlockSpec((NEW_TOKENS, HQ * HD), lambda i: (0, 0)),
        compiler_params=pltpu.CompilerParams(vmem_limit_bytes=32 * 2**20),
    )(used, queries, suffix_kv, heads, heads)


def fetch_any(state_slot, kv_ids, state_pool, conv_pool, kv_pool):
    n = lax.axis_size("pool")
    maxb = kv_ids.shape[0]
    slots = lax.all_gather(state_slot, "pool", axis=0, tiled=True)
    ids = lax.all_gather(kv_ids, "pool", axis=0, tiled=True)

    def move(pool, wanted, count):
        width = pool.size // pool.shape[0] // n
        rows = pool.reshape(pool.shape[0], n, width)
        held = lax.all_to_all(rows, "pool", split_axis=1, concat_axis=0, tiled=True)
        send = held.reshape(-1, width)[wanted].reshape(n, count, 1, width)
        return lax.all_to_all(send, "pool", split_axis=0, concat_axis=2, tiled=True)

    state = move(state_pool, slots, 1).reshape(NS, DI).astype(BF)
    conv = move(conv_pool, slots, 1).reshape(KW - 1, DI)
    blocks = move(kv_pool, ids, maxb).reshape(maxb, BLK, KVW // LANES, LANES)
    state = state.reshape(NS, 8, GROUPS, LANES).transpose(1, 2, 0, 3)
    conv = conv.reshape(KW - 1, 8, GROUPS, LANES).transpose(1, 2, 0, 3)
    conv = jnp.pad(conv, ((0, 0), (0, 0), (0, 1), (0, 0)))
    st = jnp.concatenate(
        [state.reshape(8, GROUPS * NS, LANES), conv.reshape(8, CONV_ROWS, LANES)], axis=1
    )
    return st, blocks.transpose(2, 0, 1, 3)


def on_device(
    x_gate,
    dt_raw,
    state_maps,
    a_log,
    conv_weight,
    dt_bias,
    d_skip,
    state_pool,
    conv_pool,
    queries,
    suffix_kv,
    kv_pool,
    state_slot,
    kv_ids,
    prefix_blocks,
):
    inputs = (x_gate[0, 0], dt_raw[0, 0], state_maps[0, 0])
    params = (a_log[0], conv_weight[0], dt_bias[0], d_skip[0])
    cache = (state_slot[0], kv_ids[0, 0], state_pool[0], conv_pool[0], kv_pool[0])
    if lax.axis_size("pool") == DI // PIECE:
        mixed_out, last_state, heads = serve(*cache, *inputs, *params)
    else:
        st, heads = fetch_any(*cache)
        mixed_out, last_state = mixer(*inputs, *params, st)
    attended = attend(queries[0, 0], suffix_kv[0, 0], heads, prefix_blocks[0])
    return (mixed_out[None, None], last_state[None, None], attended[None, None])


def solution(mesh):
    placed = (
        P("section", ("groups", "pool"), None, None),
        P("section", ("groups", "pool"), None, None),
        P("section", ("groups", "pool"), None, None),
        P("section", None, None),
        P("section", None, None),
        P("section", None),
        P("section", None),
        P("section", ("groups", "pool"), None, None),
        P("section", ("groups", "pool"), None, None),
        P("section", ("groups", "pool"), None, None),
        P("section", ("groups", "pool"), None, None),
        P("section", ("groups", "pool"), None, None),
        P("section", ("groups", "pool")),
        P("section", ("groups", "pool"), None),
        P("section", ("groups", "pool")),
    )
    return jax.shard_map(
        on_device,
        mesh=mesh,
        in_specs=placed,
        out_specs=(
            P("section", ("groups", "pool"), None, None),
            P("section", ("groups", "pool"), None, None),
            P("section", ("groups", "pool"), None, None),
        ),
        check_vma=False,
    )
```

```python
import functools
import math

import jax
import jax.numpy as jnp
from jax import lax
from jax.experimental import pallas as pl
from jax.experimental.pallas import tpu as pltpu
from jax.sharding import PartitionSpec as P

DI = 8192
NS = 16
KW = 4
HD = 128
HQ = 16
HK = 4
NEW_TOKENS = 128
BLK = 64
KVW = 1024
LANES = 128
LIVE = 4
PIECE = DI // 8
GROUPS = PIECE // LANES
CONV_ROWS = 32
ST_ROWS = GROUPS * NS + CONV_ROWS
LOG2E = math.log2(math.e)
MESH = pl.DeviceIdType.MESH
BF = jnp.bfloat16
F32 = jnp.float32


CHUNKS = 2


def mix(i, maps_ref, a_ref, w_ref, skip_ref, x_ref, st_ref, out_ref, last_ref,
        rate_s, gate_s, drive_s, y_s, sig_s, a_s, h_s, u_s):
    tokens = NEW_TOKENS
    width = CHUNKS * PIECE

    def columns(q, j):
        return pl.ds(pl.multiple_of(i * width + (q * GROUPS + j) * LANES, LANES), LANES)

    for q in range(CHUNKS):
        p = i * CHUNKS + q
        conv_rows = st_ref[p, GROUPS * NS :, :].astype(F32)
        for j in range(GROUPS):
            col = columns(q, j)
            here = (q * GROUPS + j) * LANES
            u_s[5:8, :] = conv_rows[KW * j : KW * j + KW - 1]
            u_s[8:, :] = x_ref[:, col].astype(F32)
            acc = w_ref[0:1, col] * u_s[5 : 5 + tokens, :]
            for k in range(1, KW):
                acc = acc + w_ref[k : k + 1, col] * u_s[5 + k : 5 + k + tokens, :]
            signal = acc / (1.0 + jnp.exp(-acc))
            sig_s[:, here : here + LANES] = signal
            rate = rate_s[p, pl.ds(j, tokens, stride=8), :]
            drive_s[q, pl.ds(j, tokens, stride=8), :] = rate * signal
            a_s[pl.ds(q * 8 + j, NS, stride=8 * CHUNKS), :] = -LOG2E * jnp.exp(a_ref[:, col])
            h_s[pl.ds(q * 8 + j, NS, stride=8 * CHUNKS), :] = st_ref[
                p, j * NS : (j + 1) * NS, :
            ].astype(F32)

    tall = 8 * CHUNKS

    def step(t, state):
        rows = pl.ds(pl.multiple_of(t * 8, 8), 8)
        rate = jnp.concatenate([rate_s[i * CHUNKS + q, rows, :] for q in range(CHUNKS)], axis=0)
        drive = jnp.concatenate([drive_s[q, rows, :] for q in range(CHUNKS)], axis=0)
        total = None
        new = []
        for m in range(NS):
            b = maps_ref[t, m]
            c = maps_ref[t, NS + m]
            decay = jnp.exp2(rate * a_s[m * tall : (m + 1) * tall, :])
            h = decay * state[m] + drive * b
            new.append(h)
            total = c * h if total is None else total + c * h
        for q in range(CHUNKS):
            y_s[q, rows, :] = total[q * 8 : (q + 1) * 8]
        return tuple(new)

    first = tuple(h_s[m * tall : (m + 1) * tall, :] for m in range(NS))
    last = lax.fori_loop(0, tokens, step, first, unroll=2)
    for m in range(NS):
        h_s[m * tall : (m + 1) * tall, :] = last[m]
    for q in range(CHUNKS):
        for j in range(GROUPS):
            col = columns(q, j)
            here = (q * GROUPS + j) * LANES
            last_ref[:, col] = h_s[pl.ds(q * 8 + j, NS, stride=tall), :]
            y = y_s[q, pl.ds(j, tokens, stride=8), :] + skip_ref[:, col] * sig_s[:, here : here + LANES]
            out_ref[:, col] = (y * gate_s[:, col]).astype(BF)


def serve_kernel(
    n,
    ids_ref,
    maps_ref,
    conv_ref,
    state_hbm,
    kv_hbm,
    dt_hbm,
    bias_hbm,
    x_hbm,
    w_hbm,
    a_hbm,
    skip_hbm,
    out_hbm,
    last_hbm,
    kv_out,
    state_ref,
    kv_ref,
    dt_ref,
    bias_ref,
    x_ref,
    w_ref,
    a_ref,
    skip_ref,
    out_ref,
    last_ref,
    st_out,
    ids_all,
    ids_s,
    table,
    table_s,
    st_send,
    st_hold,
    st_send2,
    kv_send,
    kv_hold,
    kv_send2,
    rate_s,
    gate_s,
    drive_s,
    y_s,
    sig_s,
    a_s,
    h_s,
    u_s,
    store_sem,
    local_sem,
    send_sem,
    recv_sem,
):
    me = lax.axis_index("pool")
    slots_here = state_ref.shape[0]
    blocks_here = kv_ref.shape[0]
    maxb = kv_out.shape[1]

    loads = [
        pltpu.make_async_copy(src, dst, local_sem.at[2 + i])
        for i, (src, dst) in enumerate(
            (
                (state_hbm, state_ref),
                (kv_hbm, kv_ref),
                (dt_hbm, dt_ref),
                (bias_hbm, bias_ref),
                (x_hbm, x_ref),
                (w_hbm, w_ref),
                (a_hbm, a_ref),
                (skip_hbm, skip_ref),
            )
        )
    ]
    for copy in loads:
        copy.start()

    barrier = pltpu.get_barrier_semaphore()
    for k in range(1, n):
        pl.semaphore_signal(
            barrier, inc=1, device_id={"pool": lax.rem(me + k, n)}, device_id_type=MESH
        )
    pl.semaphore_wait(barrier, n - 1)

    def push(kind, k, src, dst):
        copy = pltpu.make_async_remote_copy(
            src_ref=src,
            dst_ref=dst,
            send_sem=send_sem.at[kind, k],
            recv_sem=recv_sem.at[kind, k],
            device_id={"pool": lax.rem(me + k, n)},
            device_id_type=MESH,
        )
        copy.start()
        return copy

    def peer(k):
        return lax.rem(me + k, n)

    copies = [push(0, k, ids_ref, ids_all.at[me]) for k in range(1, n)]
    ids_all[me] = ids_ref[...]
    for copy in copies:
        copy.wait()

    lane = lax.broadcasted_iota(jnp.int32, (8, LANES), 1)
    hit = jnp.zeros((8, LANES), jnp.int32)
    for r in range(n):
        hit = jnp.maximum(hit, (ids_all[r, :maxb] == lane).astype(jnp.int32))
    named = jnp.broadcast_to(jnp.max(hit, axis=0, keepdims=True), (8, LANES))
    rank = jnp.zeros((8, LANES), jnp.int32)
    inner = lax.rem(lane, blocks_here)
    for d in range(1, blocks_here):
        rank = rank + jnp.where(inner >= d, pltpu.roll(named, d, axis=1), 0)
    table[0:8] = named
    table[8:16] = rank
    to_s = [
        pltpu.make_async_copy(ids_all, ids_s, local_sem.at[0]),
        pltpu.make_async_copy(table, table_s, local_sem.at[1]),
    ]
    for copy in to_s:
        copy.start()
    for copy in to_s:
        copy.wait()

    slot = jnp.int32(0)
    for r in range(n):
        rel = ids_s[r, maxb, 0] - me * slots_here
        slot = jnp.where((rel >= 0) & (rel < slots_here), rel, slot)
    live = [jnp.int32(0)] * LIVE
    for j in range(blocks_here):
        is_named = table_s[0, me * blocks_here + j]
        at = table_s[8, me * blocks_here + j]
        for k in range(LIVE):
            live[k] = jnp.where((is_named == 1) & (at == k), j, live[k])

    loads[0].wait()
    for p in range(n):
        for j in range(GROUPS):
            lo = (p * GROUPS + j) * LANES
            st_send[p, j * NS : (j + 1) * NS, :] = state_ref[slot, :, lo : lo + LANES].astype(BF)
        st_send[p, GROUPS * NS :, :] = conv_ref[slot, p]
    st_first = [push(1, k, st_send.at[peer(k)], st_hold.at[me]) for k in range(1, n)]
    st_hold[me] = st_send[me]

    loads[2].wait()
    loads[3].wait()

    def rates(p, carry):
        for j in range(GROUPS):
            col = pl.ds(pl.multiple_of(p * PIECE + j * LANES, LANES), LANES)
            v = dt_ref[:, col].astype(F32) + bias_ref[:, col]
            rate = jnp.maximum(v, 0.0) + jnp.log1p(jnp.exp(-jnp.abs(v)))
            rate_s[p, pl.ds(j, NEW_TOKENS, stride=8), :] = rate
        return carry

    lax.fori_loop(0, DI // PIECE, rates, 0)

    for copy in st_first:
        copy.wait()
    st_second = []
    for k in range(1, n):
        owner = ids_s[peer(k), maxb, 0] // slots_here
        st_send2[k] = st_hold[owner]
        st_second.append(push(3, k, st_send2.at[k], st_out.at[me]))
    st_out[me] = st_hold[ids_s[me, maxb, 0] // slots_here]

    loads[1].wait()
    for p in range(n):
        for k in range(LIVE):
            kv_send[p, k] = kv_ref[live[k], :, p * LANES : (p + 1) * LANES]
    kv_first = [push(2, k, kv_send.at[peer(k)], kv_hold.at[me]) for k in range(1, n)]
    kv_hold[me] = kv_send[me]

    for copy in loads[4:]:
        copy.wait()

    def gates(p, carry):
        for j in range(GROUPS):
            col = pl.ds(pl.multiple_of(p * PIECE + j * LANES, LANES), LANES)
            far = pl.ds(pl.multiple_of(DI + p * PIECE + j * LANES, LANES), LANES)
            gate = x_ref[:, far].astype(F32)
            gate_s[:, col] = gate / (1.0 + jnp.exp(-gate))
        return carry

    lax.fori_loop(0, DI // PIECE, gates, 0)
    for copy in st_second:
        copy.wait()

    def stores(i):
        width = CHUNKS * PIECE
        col = pl.ds(i * width if isinstance(i, int) else pl.multiple_of(i * width, width), width)
        return (
            pltpu.make_async_copy(out_ref.at[:, col], out_hbm.at[:, col], store_sem.at[0, i]),
            pltpu.make_async_copy(last_ref.at[:, col], last_hbm.at[:, col], store_sem.at[1, i]),
        )

    def run(i, carry):
        mix(i, maps_ref, a_ref, w_ref, skip_ref, x_ref, st_out, out_ref, last_ref,
            rate_s, gate_s, drive_s, y_s, sig_s, a_s, h_s, u_s)
        for copy in stores(i):
            copy.start()
        return carry

    run(0, 0)
    for copy in kv_first:
        copy.wait()
    kv_second = []
    for k in range(1, n):
        for i in range(maxb):
            block = ids_s[peer(k), i, 0]
            kv_send2[k, i] = kv_hold[block // blocks_here, table_s[8, block]]
        kv_second.append(push(4, k, kv_send2.at[k], kv_out.at[me]))
    for i in range(maxb):
        block = ids_s[me, i, 0]
        kv_out[me, i] = kv_hold[block // blocks_here, table_s[8, block]]
    lax.fori_loop(1, DI // (CHUNKS * PIECE), run, 0)
    for copy in kv_second:
        copy.wait()
    for i in range(DI // (CHUNKS * PIECE)):
        for copy in stores(i):
            copy.wait()


def serve(
    state_slot, kv_ids, state_pool, conv_pool, kv_pool, x_gate, dt_raw, state_maps, a_log, conv_weight, dt_bias, d_skip
):
    n = lax.axis_size("pool")
    maxb = kv_ids.shape[0]
    ids = jnp.concatenate(
        [
            jnp.broadcast_to(kv_ids[:, None], (maxb, LANES)),
            jnp.broadcast_to(state_slot, (8, LANES)),
        ],
        axis=0,
    )
    slots = conv_pool.shape[0]
    conv = conv_pool.reshape(slots, KW - 1, n, GROUPS, LANES).transpose(0, 2, 3, 1, 4)
    conv = jnp.pad(conv, ((0, 0), (0, 0), (0, 0), (0, 1), (0, 0)))
    conv = conv.reshape(slots, n, CONV_ROWS, LANES)
    vmem = pl.BlockSpec(memory_space=pltpu.VMEM)
    hbm = pl.BlockSpec(memory_space=pl.ANY)
    return pl.pallas_call(
        functools.partial(serve_kernel, n),
        out_shape=(
            jax.ShapeDtypeStruct((NEW_TOKENS, DI), BF),
            jax.ShapeDtypeStruct((NS, DI), F32),
            jax.ShapeDtypeStruct((n, maxb, BLK, LANES), BF),
        ),
        in_specs=[vmem, pl.BlockSpec(memory_space=pltpu.SMEM)]
        + [vmem]
        + [hbm] * 8,
        out_specs=(hbm, hbm, vmem),
        scratch_shapes=[
            pltpu.VMEM(state_pool.shape, F32),
            pltpu.VMEM(kv_pool.shape, BF),
            pltpu.VMEM(dt_raw.shape, BF),
            pltpu.VMEM((1, DI), F32),
            pltpu.VMEM(x_gate.shape, BF),
            pltpu.VMEM(conv_weight.shape, F32),
            pltpu.VMEM(a_log.shape, F32),
            pltpu.VMEM((1, DI), F32),
            pltpu.VMEM((NEW_TOKENS, DI), BF),
            pltpu.VMEM((NS, DI), F32),
            pltpu.VMEM((n, ST_ROWS, LANES), BF),
            pltpu.VMEM((n, maxb + 8, LANES), jnp.int32),
            pltpu.SMEM((n, maxb + 8, LANES), jnp.int32),
            pltpu.VMEM((16, LANES), jnp.int32),
            pltpu.SMEM((16, LANES), jnp.int32),
            pltpu.VMEM((n, ST_ROWS, LANES), BF),
            pltpu.VMEM((n, ST_ROWS, LANES), BF),
            pltpu.VMEM((n, ST_ROWS, LANES), BF),
            pltpu.VMEM((n, LIVE, BLK, LANES), BF),
            pltpu.VMEM((n, LIVE, BLK, LANES), BF),
            pltpu.VMEM((n, maxb, BLK, LANES), BF),
            pltpu.VMEM((DI // PIECE, NEW_TOKENS * 8, LANES), F32),
            pltpu.VMEM((NEW_TOKENS, DI), F32),
            pltpu.VMEM((CHUNKS, NEW_TOKENS * 8, LANES), F32),
            pltpu.VMEM((CHUNKS, NEW_TOKENS * 8, LANES), F32),
            pltpu.VMEM((NEW_TOKENS, CHUNKS * PIECE), F32),
            pltpu.VMEM((CHUNKS * NS * 8, LANES), F32),
            pltpu.VMEM((CHUNKS * NS * 8, LANES), F32),
            pltpu.VMEM((NEW_TOKENS + 8, LANES), F32),
            pltpu.SemaphoreType.DMA((2, DI // (CHUNKS * PIECE))),
            pltpu.SemaphoreType.DMA((10,)),
            pltpu.SemaphoreType.DMA((5, n)),
            pltpu.SemaphoreType.DMA((5, n)),
        ],
        compiler_params=pltpu.CompilerParams(
            collective_id=0, has_side_effects=True, vmem_limit_bytes=52 * 2**20
        ),
    )(
        ids,
        state_maps.astype(F32),
        conv,
        state_pool,
        kv_pool,
        dt_raw,
        dt_bias[None],
        x_gate,
        conv_weight,
        a_log,
        d_skip[None],
    )


def mixer_kernel(
    x_ref,
    g_ref,
    dt_ref,
    maps_ref,
    a_ref,
    w_ref,
    bias_ref,
    skip_ref,
    st_ref,
    out_ref,
    last_ref,
    rate_s,
    drive_s,
    y_s,
    sig_s,
    a_s,
    h_s,
    u_s,
):
    tokens = NEW_TOKENS
    for q in range(CHUNKS):
        conv_rows = st_ref[q, GROUPS * NS :, :].astype(F32)
        for j in range(GROUPS):
            col = pl.ds((q * GROUPS + j) * LANES, LANES)
            u_s[5:8, :] = conv_rows[KW * j : KW * j + KW - 1]
            u_s[8:, :] = x_ref[:, col].astype(F32)
            acc = w_ref[0:1, col] * u_s[5 : 5 + tokens, :]
            for k in range(1, KW):
                acc = acc + w_ref[k : k + 1, col] * u_s[5 + k : 5 + k + tokens, :]
            signal = acc / (1.0 + jnp.exp(-acc))
            v = dt_ref[:, col].astype(F32) + bias_ref[:, col]
            rate = jnp.maximum(v, 0.0) + jnp.log1p(jnp.exp(-jnp.abs(v)))
            sig_s[:, col] = signal
            rate_s[q, pl.ds(j, tokens, stride=8), :] = rate
            drive_s[q, pl.ds(j, tokens, stride=8), :] = rate * signal
            a_s[q, pl.ds(j, NS, stride=8), :] = -LOG2E * jnp.exp(a_ref[:, col])
            h_s[q, pl.ds(j, NS, stride=8), :] = st_ref[q, j * NS : (j + 1) * NS, :].astype(F32)

    def step(t, state):
        rows = pl.ds(pl.multiple_of(t * 8, 8), 8)
        rate = [rate_s[q, rows, :] for q in range(CHUNKS)]
        drive = [drive_s[q, rows, :] for q in range(CHUNKS)]
        total = [None] * CHUNKS
        new = []
        for m in range(NS):
            b = maps_ref[t, m]
            c = maps_ref[t, NS + m]
            for q in range(CHUNKS):
                decay = jnp.exp2(rate[q] * a_s[q, m * 8 : (m + 1) * 8, :])
                h = decay * state[m * CHUNKS + q] + drive[q] * b
                new.append(h)
                total[q] = c * h if total[q] is None else total[q] + c * h
        for q in range(CHUNKS):
            y_s[q, rows, :] = total[q]
        return tuple(new)

    first = tuple(
        h_s[q, m * 8 : (m + 1) * 8, :] for m in range(NS) for q in range(CHUNKS)
    )
    last = lax.fori_loop(0, tokens, step, first, unroll=2)
    for m in range(NS):
        for q in range(CHUNKS):
            h_s[q, m * 8 : (m + 1) * 8, :] = last[m * CHUNKS + q]
    for q in range(CHUNKS):
        for j in range(GROUPS):
            col = pl.ds((q * GROUPS + j) * LANES, LANES)
            last_ref[:, col] = h_s[q, pl.ds(j, NS, stride=8), :]
            gate = g_ref[:, col].astype(F32)
            y = y_s[q, pl.ds(j, tokens, stride=8), :] + skip_ref[:, col] * sig_s[:, col]
            out_ref[:, col] = (y * (gate / (1.0 + jnp.exp(-gate)))).astype(BF)


def mixer(x_gate, dt_raw, state_maps, a_log, conv_weight, dt_bias, d_skip, st):
    width = CHUNKS * PIECE
    steps = DI // width
    t = NEW_TOKENS
    return pl.pallas_call(
        mixer_kernel,
        grid=(steps,),
        out_shape=(
            jax.ShapeDtypeStruct((t, DI), BF),
            jax.ShapeDtypeStruct((NS, DI), F32),
        ),
        in_specs=[
            pl.BlockSpec((t, width), lambda i: (0, i)),
            pl.BlockSpec((t, width), lambda i: (0, i + steps)),
            pl.BlockSpec((t, width), lambda i: (0, i)),
            pl.BlockSpec(memory_space=pltpu.SMEM),
            pl.BlockSpec((NS, width), lambda i: (0, i)),
            pl.BlockSpec((KW, width), lambda i: (0, i)),
            pl.BlockSpec((1, width), lambda i: (0, i)),
            pl.BlockSpec((1, width), lambda i: (0, i)),
            pl.BlockSpec((CHUNKS, ST_ROWS, LANES), lambda i: (i, 0, 0)),
        ],
        out_specs=(
            pl.BlockSpec((t, width), lambda i: (0, i)),
            pl.BlockSpec((NS, width), lambda i: (0, i)),
        ),
        scratch_shapes=[
            pltpu.VMEM((CHUNKS, t * 8, LANES), F32),
            pltpu.VMEM((CHUNKS, t * 8, LANES), F32),
            pltpu.VMEM((CHUNKS, t * 8, LANES), F32),
            pltpu.VMEM((t, width), F32),
            pltpu.VMEM((CHUNKS, NS * 8, LANES), F32),
            pltpu.VMEM((CHUNKS, NS * 8, LANES), F32),
            pltpu.VMEM((t + 8, LANES), F32),
        ],
        compiler_params=pltpu.CompilerParams(vmem_limit_bytes=32 * 2**20),
        cost_estimate=pl.CostEstimate(
            flops=8 * t * DI * NS, bytes_accessed=10 * t * DI, transcendentals=t * DI * NS
        ),
    )(
        x_gate,
        x_gate,
        dt_raw,
        state_maps.astype(F32),
        a_log,
        conv_weight,
        dt_bias[None],
        d_skip[None],
        st,
    )


def attend_kernel(used_ref, q_ref, new_ref, k_ref, v_ref, out_ref):
    group = HQ // HK
    rows = group * NEW_TOKENS
    prefix = k_ref.shape[1] * BLK
    scale = 1.0 / math.sqrt(HD)
    used = used_ref[0]
    dims = (((1,), (1,)), ((), ()))
    for g in range(HK):
        q = jnp.concatenate(
            [q_ref[:, (g * group + i) * HD : (g * group + i + 1) * HD] for i in range(group)], axis=0
        )
        old_k = k_ref[g].reshape(prefix, HD)
        old_v = v_ref[g].reshape(prefix, HD)
        new_k = new_ref[:, g * HD : (g + 1) * HD]
        new_v = new_ref[:, (HK + g) * HD : (HK + g + 1) * HD]
        s_old = lax.dot_general(q, old_k, dims, preferred_element_type=F32) * scale
        s_new = lax.dot_general(q, new_k, dims, preferred_element_type=F32) * scale
        at = lax.broadcasted_iota(jnp.int32, (rows, prefix), 1)
        s_old = jnp.where(at < used * BLK, s_old, -1e30)
        key = lax.broadcasted_iota(jnp.int32, (rows, NEW_TOKENS), 1)
        query = lax.broadcasted_iota(jnp.int32, (rows, NEW_TOKENS), 0) % NEW_TOKENS
        s_new = jnp.where(key <= query, s_new, -1e30)
        top = jnp.maximum(
            jnp.max(s_old, axis=1, keepdims=True), jnp.max(s_new, axis=1, keepdims=True)
        )
        w_old = jnp.exp(s_old - top)
        w_new = jnp.exp(s_new - top)
        norm = 1.0 / (
            jnp.sum(w_old, axis=1, keepdims=True) + jnp.sum(w_new, axis=1, keepdims=True)
        )
        mixed = jnp.dot((w_old * norm).astype(BF), old_v, preferred_element_type=F32)
        mixed = mixed + jnp.dot((w_new * norm).astype(BF), new_v, preferred_element_type=F32)
        for i in range(group):
            out_ref[:, (g * group + i) * HD : (g * group + i + 1) * HD] = mixed[
                i * NEW_TOKENS : (i + 1) * NEW_TOKENS
            ].astype(BF)


def attend(queries, suffix_kv, heads, used):
    maxb = heads.shape[1]
    return pl.pallas_call(
        attend_kernel,
        grid=(1,),
        out_shape=jax.ShapeDtypeStruct((NEW_TOKENS, HQ * HD), BF),
        in_specs=[
            pl.BlockSpec(memory_space=pltpu.SMEM),
            pl.BlockSpec((NEW_TOKENS, HQ * HD), lambda i: (0, 0)),
            pl.BlockSpec((NEW_TOKENS, KVW), lambda i: (0, 0)),
            pl.BlockSpec((HK, maxb, BLK, HD), lambda i: (0, 0, 0, 0)),
            pl.BlockSpec((HK, maxb, BLK, HD), lambda i: (1, 0, 0, 0)),
        ],
        out_specs=pl.BlockSpec((NEW_TOKENS, HQ * HD), lambda i: (0, 0)),
        compiler_params=pltpu.CompilerParams(vmem_limit_bytes=32 * 2**20),
    )(used, queries, suffix_kv, heads, heads)


def fetch_any(state_slot, kv_ids, state_pool, conv_pool, kv_pool):
    n = lax.axis_size("pool")
    maxb = kv_ids.shape[0]
    slots = lax.all_gather(state_slot, "pool", axis=0, tiled=True)
    ids = lax.all_gather(kv_ids, "pool", axis=0, tiled=True)

    def move(pool, wanted, count):
        width = pool.size // pool.shape[0] // n
        rows = pool.reshape(pool.shape[0], n, width)
        held = lax.all_to_all(rows, "pool", split_axis=1, concat_axis=0, tiled=True)
        send = held.reshape(-1, width)[wanted].reshape(n, count, 1, width)
        return lax.all_to_all(send, "pool", split_axis=0, concat_axis=2, tiled=True)

    state = move(state_pool, slots, 1).reshape(NS, DI).astype(BF)
    conv = move(conv_pool, slots, 1).reshape(KW - 1, DI)
    blocks = move(kv_pool, ids, maxb).reshape(maxb, BLK, KVW // LANES, LANES)
    state = state.reshape(NS, 8, GROUPS, LANES).transpose(1, 2, 0, 3)
    conv = conv.reshape(KW - 1, 8, GROUPS, LANES).transpose(1, 2, 0, 3)
    conv = jnp.pad(conv, ((0, 0), (0, 0), (0, 1), (0, 0)))
    st = jnp.concatenate(
        [state.reshape(8, GROUPS * NS, LANES), conv.reshape(8, CONV_ROWS, LANES)], axis=1
    )
    return st, blocks.transpose(2, 0, 1, 3)


def on_device(
    x_gate,
    dt_raw,
    state_maps,
    a_log,
    conv_weight,
    dt_bias,
    d_skip,
    state_pool,
    conv_pool,
    queries,
    suffix_kv,
    kv_pool,
    state_slot,
    kv_ids,
    prefix_blocks,
):
    inputs = (x_gate[0, 0], dt_raw[0, 0], state_maps[0, 0])
    params = (a_log[0], conv_weight[0], dt_bias[0], d_skip[0])
    cache = (state_slot[0], kv_ids[0, 0], state_pool[0], conv_pool[0], kv_pool[0])
    if lax.axis_size("pool") == DI // PIECE:
        mixed_out, last_state, heads = serve(*cache, *inputs, *params)
    else:
        st, heads = fetch_any(*cache)
        mixed_out, last_state = mixer(*inputs, *params, st)
    attended = attend(queries[0, 0], suffix_kv[0, 0], heads, prefix_blocks[0])
    return (mixed_out[None, None], last_state[None, None], attended[None, None])


def solution(mesh):
    placed = (
        P("section", ("groups", "pool"), None, None),
        P("section", ("groups", "pool"), None, None),
        P("section", ("groups", "pool"), None, None),
        P("section", None, None),
        P("section", None, None),
        P("section", None),
        P("section", None),
        P("section", ("groups", "pool"), None, None),
        P("section", ("groups", "pool"), None, None),
        P("section", ("groups", "pool"), None, None),
        P("section", ("groups", "pool"), None, None),
        P("section", ("groups", "pool"), None, None),
        P("section", ("groups", "pool")),
        P("section", ("groups", "pool"), None),
        P("section", ("groups", "pool")),
    )
    return jax.shard_map(
        on_device,
        mesh=mesh,
        in_specs=placed,
        out_specs=(
            P("section", ("groups", "pool"), None, None),
            P("section", ("groups", "pool"), None, None),
            P("section", ("groups", "pool"), None, None),
        ),
        check_vma=False,
    )
```

```python
import functools
import math

import jax
import jax.numpy as jnp
from jax import lax
from jax.experimental import pallas as pl
from jax.experimental.pallas import tpu as pltpu
from jax.sharding import PartitionSpec as P

DI = 8192
NS = 16
KW = 4
HD = 128
HQ = 16
HK = 4
NEW_TOKENS = 128
BLK = 64
KVW = 1024
LANES = 128
LIVE = 4
PIECE = DI // 8
GROUPS = PIECE // LANES
CONV_ROWS = 32
ST_ROWS = GROUPS * NS + CONV_ROWS
LOG2E = math.log2(math.e)
MESH = pl.DeviceIdType.MESH
BF = jnp.bfloat16
F32 = jnp.float32


CHUNKS = 2


def silu(v):
    half = 0.5 * v
    return half + half * jnp.tanh(half)


def mix(i, maps_ref, a_ref, w_ref, skip_ref, x_ref, st_ref, out_ref, last_ref,
        rate_s, gate_s, drive_s, y_s, sig_s, a_s, h_s, u_s):
    tokens = NEW_TOKENS
    width = CHUNKS * PIECE

    def columns(q, j):
        return pl.ds(pl.multiple_of(i * width + (q * GROUPS + j) * LANES, LANES), LANES)

    for q in range(CHUNKS):
        p = i * CHUNKS + q
        conv_rows = st_ref[p, GROUPS * NS :, :].astype(F32)
        for j in range(GROUPS):
            col = columns(q, j)
            here = (q * GROUPS + j) * LANES
            u_s[5:8, :] = conv_rows[KW * j : KW * j + KW - 1]
            u_s[8:, :] = x_ref[:, col].astype(F32)
            acc = w_ref[0:1, col] * u_s[5 : 5 + tokens, :]
            for k in range(1, KW):
                acc = acc + w_ref[k : k + 1, col] * u_s[5 + k : 5 + k + tokens, :]
            signal = silu(acc)
            sig_s[:, here : here + LANES] = signal
            rate = rate_s[p, pl.ds(j, tokens, stride=8), :]
            drive_s[q, pl.ds(j, tokens, stride=8), :] = rate * signal
            a_s[pl.ds(q * 8 + j, NS, stride=8 * CHUNKS), :] = -LOG2E * jnp.exp(a_ref[:, col])
            h_s[pl.ds(q * 8 + j, NS, stride=8 * CHUNKS), :] = st_ref[
                p, j * NS : (j + 1) * NS, :
            ].astype(F32)

    tall = 8 * CHUNKS

    def step(t, state):
        rows = pl.ds(pl.multiple_of(t * 8, 8), 8)
        rate = jnp.concatenate([rate_s[i * CHUNKS + q, rows, :] for q in range(CHUNKS)], axis=0)
        drive = jnp.concatenate([drive_s[q, rows, :] for q in range(CHUNKS)], axis=0)
        total = None
        new = []
        for m in range(NS):
            b = maps_ref[t, m]
            c = maps_ref[t, NS + m]
            decay = jnp.exp2(rate * a_s[m * tall : (m + 1) * tall, :])
            h = decay * state[m] + drive * b
            new.append(h)
            total = c * h if total is None else total + c * h
        for q in range(CHUNKS):
            y_s[q, rows, :] = total[q * 8 : (q + 1) * 8]
        return tuple(new)

    first = tuple(h_s[m * tall : (m + 1) * tall, :] for m in range(NS))
    last = lax.fori_loop(0, tokens, step, first, unroll=2)
    for m in range(NS):
        h_s[m * tall : (m + 1) * tall, :] = last[m]
    for q in range(CHUNKS):
        for j in range(GROUPS):
            col = columns(q, j)
            here = (q * GROUPS + j) * LANES
            last_ref[:, col] = h_s[pl.ds(q * 8 + j, NS, stride=tall), :]
            y = y_s[q, pl.ds(j, tokens, stride=8), :] + skip_ref[:, col] * sig_s[:, here : here + LANES]
            out_ref[:, col] = (y * gate_s[:, col]).astype(BF)


def serve_kernel(
    n,
    ids_ref,
    maps_ref,
    conv_ref,
    state_hbm,
    kv_hbm,
    dt_hbm,
    bias_hbm,
    x_hbm,
    w_hbm,
    a_hbm,
    skip_hbm,
    out_hbm,
    last_hbm,
    kv_out,
    state_ref,
    kv_ref,
    dt_ref,
    bias_ref,
    x_ref,
    w_ref,
    a_ref,
    skip_ref,
    out_ref,
    last_ref,
    st_out,
    ids_all,
    ids_s,
    table,
    table_s,
    st_send,
    st_hold,
    st_send2,
    kv_send,
    kv_hold,
    kv_send2,
    rate_s,
    gate_s,
    drive_s,
    y_s,
    sig_s,
    a_s,
    h_s,
    u_s,
    store_sem,
    local_sem,
    send_sem,
    recv_sem,
):
    me = lax.axis_index("pool")
    slots_here = state_ref.shape[0]
    blocks_here = kv_ref.shape[0]
    maxb = kv_out.shape[1]

    loads = [
        pltpu.make_async_copy(src, dst, local_sem.at[2 + i])
        for i, (src, dst) in enumerate(
            (
                (state_hbm, state_ref),
                (kv_hbm, kv_ref),
                (dt_hbm, dt_ref),
                (bias_hbm, bias_ref),
                (x_hbm, x_ref),
                (w_hbm, w_ref),
                (a_hbm, a_ref),
                (skip_hbm, skip_ref),
            )
        )
    ]
    for copy in loads:
        copy.start()

    barrier = pltpu.get_barrier_semaphore()
    for k in range(1, n):
        pl.semaphore_signal(
            barrier, inc=1, device_id={"pool": lax.rem(me + k, n)}, device_id_type=MESH
        )
    pl.semaphore_wait(barrier, n - 1)

    def push(kind, k, src, dst):
        copy = pltpu.make_async_remote_copy(
            src_ref=src,
            dst_ref=dst,
            send_sem=send_sem.at[kind, k],
            recv_sem=recv_sem.at[kind, k],
            device_id={"pool": lax.rem(me + k, n)},
            device_id_type=MESH,
        )
        copy.start()
        return copy

    def peer(k):
        return lax.rem(me + k, n)

    copies = [push(0, k, ids_ref, ids_all.at[me]) for k in range(1, n)]
    ids_all[me] = ids_ref[...]

    loads[2].wait()
    loads[3].wait()

    def rates(p, carry):
        for j in range(GROUPS):
            col = pl.ds(pl.multiple_of(p * PIECE + j * LANES, LANES), LANES)
            v = dt_ref[:, col].astype(F32) + bias_ref[:, col]
            rate = jnp.maximum(v, 0.0) + jnp.log(1.0 + jnp.exp(-jnp.abs(v)))
            rate_s[p, pl.ds(j, NEW_TOKENS, stride=8), :] = rate
        return carry

    lax.fori_loop(0, DI // PIECE, rates, 0)

    for copy in copies:
        copy.wait()

    lane = lax.broadcasted_iota(jnp.int32, (8, LANES), 1)
    hit = jnp.zeros((8, LANES), jnp.int32)
    for r in range(n):
        hit = jnp.maximum(hit, (ids_all[r, :maxb] == lane).astype(jnp.int32))
    named = jnp.broadcast_to(jnp.max(hit, axis=0, keepdims=True), (8, LANES))
    rank = jnp.zeros((8, LANES), jnp.int32)
    inner = lax.rem(lane, blocks_here)
    for d in range(1, blocks_here):
        rank = rank + jnp.where(inner >= d, pltpu.roll(named, d, axis=1), 0)
    table[0:8] = named
    table[8:16] = rank
    to_s = [
        pltpu.make_async_copy(ids_all, ids_s, local_sem.at[0]),
        pltpu.make_async_copy(table, table_s, local_sem.at[1]),
    ]
    for copy in to_s:
        copy.start()
    for copy in to_s:
        copy.wait()

    slot = jnp.int32(0)
    for r in range(n):
        rel = ids_s[r, maxb, 0] - me * slots_here
        slot = jnp.where((rel >= 0) & (rel < slots_here), rel, slot)
    live = [jnp.int32(0)] * LIVE
    for j in range(blocks_here):
        is_named = table_s[0, me * blocks_here + j]
        at = table_s[8, me * blocks_here + j]
        for k in range(LIVE):
            live[k] = jnp.where((is_named == 1) & (at == k), j, live[k])

    loads[0].wait()
    for p in range(n):
        for j in range(GROUPS):
            lo = (p * GROUPS + j) * LANES
            st_send[p, j * NS : (j + 1) * NS, :] = state_ref[slot, :, lo : lo + LANES].astype(BF)
        st_send[p, GROUPS * NS :, :] = conv_ref[slot, p]
    st_first = [push(1, k, st_send.at[peer(k)], st_hold.at[me]) for k in range(1, n)]
    st_hold[me] = st_send[me]

    for copy in loads[4:]:
        copy.wait()

    def gates(p, carry):
        for j in range(GROUPS):
            col = pl.ds(pl.multiple_of(p * PIECE + j * LANES, LANES), LANES)
            far = pl.ds(pl.multiple_of(DI + p * PIECE + j * LANES, LANES), LANES)
            gate = x_ref[:, far].astype(F32)
            gate_s[:, col] = silu(gate)
        return carry

    lax.fori_loop(0, DI // PIECE, gates, 0)

    for copy in st_first:
        copy.wait()
    st_second = []
    for k in range(1, n):
        owner = ids_s[peer(k), maxb, 0] // slots_here
        st_send2[k] = st_hold[owner]
        st_second.append(push(3, k, st_send2.at[k], st_out.at[me]))
    st_out[me] = st_hold[ids_s[me, maxb, 0] // slots_here]

    loads[1].wait()
    for p in range(n):
        for k in range(LIVE):
            kv_send[p, k] = kv_ref[live[k], :, p * LANES : (p + 1) * LANES]
    kv_first = [push(2, k, kv_send.at[peer(k)], kv_hold.at[me]) for k in range(1, n)]
    kv_hold[me] = kv_send[me]

    for copy in st_second:
        copy.wait()

    def stores(i):
        width = CHUNKS * PIECE
        col = pl.ds(i * width if isinstance(i, int) else pl.multiple_of(i * width, width), width)
        return (
            pltpu.make_async_copy(out_ref.at[:, col], out_hbm.at[:, col], store_sem.at[0, i]),
            pltpu.make_async_copy(last_ref.at[:, col], last_hbm.at[:, col], store_sem.at[1, i]),
        )

    def run(i, carry):
        mix(i, maps_ref, a_ref, w_ref, skip_ref, x_ref, st_out, out_ref, last_ref,
            rate_s, gate_s, drive_s, y_s, sig_s, a_s, h_s, u_s)
        for copy in stores(i):
            copy.start()
        return carry

    run(0, 0)
    for copy in kv_first:
        copy.wait()
    kv_second = []
    for k in range(1, n):
        for i in range(maxb):
            block = ids_s[peer(k), i, 0]
            kv_send2[k, i] = kv_hold[block // blocks_here, table_s[8, block]]
        kv_second.append(push(4, k, kv_send2.at[k], kv_out.at[me]))
    for i in range(maxb):
        block = ids_s[me, i, 0]
        kv_out[me, i] = kv_hold[block // blocks_here, table_s[8, block]]
    lax.fori_loop(1, DI // (CHUNKS * PIECE), run, 0)
    for copy in kv_second:
        copy.wait()
    for i in range(DI // (CHUNKS * PIECE)):
        for copy in stores(i):
            copy.wait()


def serve(
    state_slot, kv_ids, state_pool, conv_pool, kv_pool, x_gate, dt_raw, state_maps, a_log, conv_weight, dt_bias, d_skip
):
    n = lax.axis_size("pool")
    maxb = kv_ids.shape[0]
    ids = jnp.concatenate(
        [
            jnp.broadcast_to(kv_ids[:, None], (maxb, LANES)),
            jnp.broadcast_to(state_slot, (8, LANES)),
        ],
        axis=0,
    )
    slots = conv_pool.shape[0]
    conv = conv_pool.reshape(slots, KW - 1, n, GROUPS, LANES).transpose(0, 2, 3, 1, 4)
    conv = jnp.pad(conv, ((0, 0), (0, 0), (0, 0), (0, 1), (0, 0)))
    conv = conv.reshape(slots, n, CONV_ROWS, LANES)
    vmem = pl.BlockSpec(memory_space=pltpu.VMEM)
    hbm = pl.BlockSpec(memory_space=pltpu.HBM)
    return pl.pallas_call(
        functools.partial(serve_kernel, n),
        out_shape=(
            jax.ShapeDtypeStruct((NEW_TOKENS, DI), BF),
            jax.ShapeDtypeStruct((NS, DI), F32),
            jax.ShapeDtypeStruct((n, maxb, BLK, LANES), BF),
        ),
        in_specs=[vmem, pl.BlockSpec(memory_space=pltpu.SMEM)]
        + [vmem]
        + [hbm] * 8,
        out_specs=(hbm, hbm, vmem),
        scratch_shapes=[
            pltpu.VMEM(state_pool.shape, F32),
            pltpu.VMEM(kv_pool.shape, BF),
            pltpu.VMEM(dt_raw.shape, BF),
            pltpu.VMEM((1, DI), F32),
            pltpu.VMEM(x_gate.shape, BF),
            pltpu.VMEM(conv_weight.shape, F32),
            pltpu.VMEM(a_log.shape, F32),
            pltpu.VMEM((1, DI), F32),
            pltpu.VMEM((NEW_TOKENS, DI), BF),
            pltpu.VMEM((NS, DI), F32),
            pltpu.VMEM((n, ST_ROWS, LANES), BF),
            pltpu.VMEM((n, maxb + 8, LANES), jnp.int32),
            pltpu.SMEM((n, maxb + 8, LANES), jnp.int32),
            pltpu.VMEM((16, LANES), jnp.int32),
            pltpu.SMEM((16, LANES), jnp.int32),
            pltpu.VMEM((n, ST_ROWS, LANES), BF),
            pltpu.VMEM((n, ST_ROWS, LANES), BF),
            pltpu.VMEM((n, ST_ROWS, LANES), BF),
            pltpu.VMEM((n, LIVE, BLK, LANES), BF),
            pltpu.VMEM((n, LIVE, BLK, LANES), BF),
            pltpu.VMEM((n, maxb, BLK, LANES), BF),
            pltpu.VMEM((DI // PIECE, NEW_TOKENS * 8, LANES), F32),
            pltpu.VMEM((NEW_TOKENS, DI), F32),
            pltpu.VMEM((CHUNKS, NEW_TOKENS * 8, LANES), F32),
            pltpu.VMEM((CHUNKS, NEW_TOKENS * 8, LANES), F32),
            pltpu.VMEM((NEW_TOKENS, CHUNKS * PIECE), F32),
            pltpu.VMEM((CHUNKS * NS * 8, LANES), F32),
            pltpu.VMEM((CHUNKS * NS * 8, LANES), F32),
            pltpu.VMEM((NEW_TOKENS + 8, LANES), F32),
            pltpu.SemaphoreType.DMA((2, DI // (CHUNKS * PIECE))),
            pltpu.SemaphoreType.DMA((10,)),
            pltpu.SemaphoreType.DMA((5, n)),
            pltpu.SemaphoreType.DMA((5, n)),
        ],
        compiler_params=pltpu.CompilerParams(
            collective_id=0, has_side_effects=True, vmem_limit_bytes=62 * 2**20
        ),
    )(
        ids,
        state_maps.astype(F32),
        conv,
        state_pool,
        kv_pool,
        dt_raw,
        dt_bias[None],
        x_gate,
        conv_weight,
        a_log,
        d_skip[None],
    )


def mixer_kernel(
    x_ref,
    g_ref,
    dt_ref,
    maps_ref,
    a_ref,
    w_ref,
    bias_ref,
    skip_ref,
    st_ref,
    out_ref,
    last_ref,
    rate_s,
    drive_s,
    y_s,
    sig_s,
    a_s,
    h_s,
    u_s,
):
    tokens = NEW_TOKENS
    for q in range(CHUNKS):
        conv_rows = st_ref[q, GROUPS * NS :, :].astype(F32)
        for j in range(GROUPS):
            col = pl.ds((q * GROUPS + j) * LANES, LANES)
            u_s[5:8, :] = conv_rows[KW * j : KW * j + KW - 1]
            u_s[8:, :] = x_ref[:, col].astype(F32)
            acc = w_ref[0:1, col] * u_s[5 : 5 + tokens, :]
            for k in range(1, KW):
                acc = acc + w_ref[k : k + 1, col] * u_s[5 + k : 5 + k + tokens, :]
            signal = silu(acc)
            v = dt_ref[:, col].astype(F32) + bias_ref[:, col]
            rate = jnp.maximum(v, 0.0) + jnp.log(1.0 + jnp.exp(-jnp.abs(v)))
            sig_s[:, col] = signal
            rate_s[q, pl.ds(j, tokens, stride=8), :] = rate
            drive_s[q, pl.ds(j, tokens, stride=8), :] = rate * signal
            a_s[q, pl.ds(j, NS, stride=8), :] = -LOG2E * jnp.exp(a_ref[:, col])
            h_s[q, pl.ds(j, NS, stride=8), :] = st_ref[q, j * NS : (j + 1) * NS, :].astype(F32)

    def step(t, state):
        rows = pl.ds(pl.multiple_of(t * 8, 8), 8)
        rate = [rate_s[q, rows, :] for q in range(CHUNKS)]
        drive = [drive_s[q, rows, :] for q in range(CHUNKS)]
        total = [None] * CHUNKS
        new = []
        for m in range(NS):
            b = maps_ref[t, m]
            c = maps_ref[t, NS + m]
            for q in range(CHUNKS):
                decay = jnp.exp2(rate[q] * a_s[q, m * 8 : (m + 1) * 8, :])
                h = decay * state[m * CHUNKS + q] + drive[q] * b
                new.append(h)
                total[q] = c * h if total[q] is None else total[q] + c * h
        for q in range(CHUNKS):
            y_s[q, rows, :] = total[q]
        return tuple(new)

    first = tuple(
        h_s[q, m * 8 : (m + 1) * 8, :] for m in range(NS) for q in range(CHUNKS)
    )
    last = lax.fori_loop(0, tokens, step, first, unroll=2)
    for m in range(NS):
        for q in range(CHUNKS):
            h_s[q, m * 8 : (m + 1) * 8, :] = last[m * CHUNKS + q]
    for q in range(CHUNKS):
        for j in range(GROUPS):
            col = pl.ds((q * GROUPS + j) * LANES, LANES)
            last_ref[:, col] = h_s[q, pl.ds(j, NS, stride=8), :]
            gate = g_ref[:, col].astype(F32)
            y = y_s[q, pl.ds(j, tokens, stride=8), :] + skip_ref[:, col] * sig_s[:, col]
            out_ref[:, col] = (y * silu(gate)).astype(BF)


def mixer(x_gate, dt_raw, state_maps, a_log, conv_weight, dt_bias, d_skip, st):
    width = CHUNKS * PIECE
    steps = DI // width
    t = NEW_TOKENS
    return pl.pallas_call(
        mixer_kernel,
        grid=(steps,),
        out_shape=(
            jax.ShapeDtypeStruct((t, DI), BF),
            jax.ShapeDtypeStruct((NS, DI), F32),
        ),
        in_specs=[
            pl.BlockSpec((t, width), lambda i: (0, i)),
            pl.BlockSpec((t, width), lambda i: (0, i + steps)),
            pl.BlockSpec((t, width), lambda i: (0, i)),
            pl.BlockSpec(memory_space=pltpu.SMEM),
            pl.BlockSpec((NS, width), lambda i: (0, i)),
            pl.BlockSpec((KW, width), lambda i: (0, i)),
            pl.BlockSpec((1, width), lambda i: (0, i)),
            pl.BlockSpec((1, width), lambda i: (0, i)),
            pl.BlockSpec((CHUNKS, ST_ROWS, LANES), lambda i: (i, 0, 0)),
        ],
        out_specs=(
            pl.BlockSpec((t, width), lambda i: (0, i)),
            pl.BlockSpec((NS, width), lambda i: (0, i)),
        ),
        scratch_shapes=[
            pltpu.VMEM((CHUNKS, t * 8, LANES), F32),
            pltpu.VMEM((CHUNKS, t * 8, LANES), F32),
            pltpu.VMEM((CHUNKS, t * 8, LANES), F32),
            pltpu.VMEM((t, width), F32),
            pltpu.VMEM((CHUNKS, NS * 8, LANES), F32),
            pltpu.VMEM((CHUNKS, NS * 8, LANES), F32),
            pltpu.VMEM((t + 8, LANES), F32),
        ],
        compiler_params=pltpu.CompilerParams(vmem_limit_bytes=32 * 2**20),
        cost_estimate=pl.CostEstimate(
            flops=8 * t * DI * NS, bytes_accessed=10 * t * DI, transcendentals=t * DI * NS
        ),
    )(
        x_gate,
        x_gate,
        dt_raw,
        state_maps.astype(F32),
        a_log,
        conv_weight,
        dt_bias[None],
        d_skip[None],
        st,
    )


def attend_kernel(used_ref, q_ref, new_ref, k_ref, v_ref, out_ref):
    group = HQ // HK
    rows = group * NEW_TOKENS
    prefix = k_ref.shape[1] * BLK
    scale = 1.0 / math.sqrt(HD)
    used = used_ref[0]
    dims = (((1,), (1,)), ((), ()))
    for g in range(HK):
        q = jnp.concatenate(
            [q_ref[:, (g * group + i) * HD : (g * group + i + 1) * HD] for i in range(group)], axis=0
        )
        old_k = k_ref[g].reshape(prefix, HD)
        old_v = v_ref[g].reshape(prefix, HD)
        new_k = new_ref[:, g * HD : (g + 1) * HD]
        new_v = new_ref[:, (HK + g) * HD : (HK + g + 1) * HD]
        s_old = lax.dot_general(q, old_k, dims, preferred_element_type=F32) * scale
        s_new = lax.dot_general(q, new_k, dims, preferred_element_type=F32) * scale
        at = lax.broadcasted_iota(jnp.int32, (rows, prefix), 1)
        s_old = jnp.where(at < used * BLK, s_old, -1e30)
        key = lax.broadcasted_iota(jnp.int32, (rows, NEW_TOKENS), 1)
        query = lax.broadcasted_iota(jnp.int32, (rows, NEW_TOKENS), 0) % NEW_TOKENS
        s_new = jnp.where(key <= query, s_new, -1e30)
        top = jnp.maximum(
            jnp.max(s_old, axis=1, keepdims=True), jnp.max(s_new, axis=1, keepdims=True)
        )
        w_old = jnp.exp(s_old - top)
        w_new = jnp.exp(s_new - top)
        norm = 1.0 / (
            jnp.sum(w_old, axis=1, keepdims=True) + jnp.sum(w_new, axis=1, keepdims=True)
        )
        mixed = jnp.dot((w_old * norm).astype(BF), old_v, preferred_element_type=F32)
        mixed = mixed + jnp.dot((w_new * norm).astype(BF), new_v, preferred_element_type=F32)
        for i in range(group):
            out_ref[:, (g * group + i) * HD : (g * group + i + 1) * HD] = mixed[
                i * NEW_TOKENS : (i + 1) * NEW_TOKENS
            ].astype(BF)


def attend(queries, suffix_kv, heads, used):
    maxb = heads.shape[1]
    return pl.pallas_call(
        attend_kernel,
        grid=(1,),
        out_shape=jax.ShapeDtypeStruct((NEW_TOKENS, HQ * HD), BF),
        in_specs=[
            pl.BlockSpec(memory_space=pltpu.SMEM),
            pl.BlockSpec((NEW_TOKENS, HQ * HD), lambda i: (0, 0)),
            pl.BlockSpec((NEW_TOKENS, KVW), lambda i: (0, 0)),
            pl.BlockSpec((HK, maxb, BLK, HD), lambda i: (0, 0, 0, 0)),
            pl.BlockSpec((HK, maxb, BLK, HD), lambda i: (1, 0, 0, 0)),
        ],
        out_specs=pl.BlockSpec((NEW_TOKENS, HQ * HD), lambda i: (0, 0)),
        compiler_params=pltpu.CompilerParams(vmem_limit_bytes=32 * 2**20),
    )(used, queries, suffix_kv, heads, heads)


def fetch_any(state_slot, kv_ids, state_pool, conv_pool, kv_pool):
    n = lax.axis_size("pool")
    maxb = kv_ids.shape[0]
    slots = lax.all_gather(state_slot, "pool", axis=0, tiled=True)
    ids = lax.all_gather(kv_ids, "pool", axis=0, tiled=True)

    def move(pool, wanted, count):
        width = pool.size // pool.shape[0] // n
        rows = pool.reshape(pool.shape[0], n, width)
        held = lax.all_to_all(rows, "pool", split_axis=1, concat_axis=0, tiled=True)
        send = held.reshape(-1, width)[wanted].reshape(n, count, 1, width)
        return lax.all_to_all(send, "pool", split_axis=0, concat_axis=2, tiled=True)

    state = move(state_pool, slots, 1).reshape(NS, DI).astype(BF)
    conv = move(conv_pool, slots, 1).reshape(KW - 1, DI)
    blocks = move(kv_pool, ids, maxb).reshape(maxb, BLK, KVW // LANES, LANES)
    state = state.reshape(NS, 8, GROUPS, LANES).transpose(1, 2, 0, 3)
    conv = conv.reshape(KW - 1, 8, GROUPS, LANES).transpose(1, 2, 0, 3)
    conv = jnp.pad(conv, ((0, 0), (0, 0), (0, 1), (0, 0)))
    st = jnp.concatenate(
        [state.reshape(8, GROUPS * NS, LANES), conv.reshape(8, CONV_ROWS, LANES)], axis=1
    )
    return st, blocks.transpose(2, 0, 1, 3)


def on_device(
    x_gate,
    dt_raw,
    state_maps,
    a_log,
    conv_weight,
    dt_bias,
    d_skip,
    state_pool,
    conv_pool,
    queries,
    suffix_kv,
    kv_pool,
    state_slot,
    kv_ids,
    prefix_blocks,
):
    inputs = (x_gate[0, 0], dt_raw[0, 0], state_maps[0, 0])
    params = (a_log[0], conv_weight[0], dt_bias[0], d_skip[0])
    cache = (state_slot[0], kv_ids[0, 0], state_pool[0], conv_pool[0], kv_pool[0])
    if lax.axis_size("pool") == DI // PIECE:
        mixed_out, last_state, heads = serve(*cache, *inputs, *params)
    else:
        st, heads = fetch_any(*cache)
        mixed_out, last_state = mixer(*inputs, *params, st)
    attended = attend(queries[0, 0], suffix_kv[0, 0], heads, prefix_blocks[0])
    return (mixed_out[None, None], last_state[None, None], attended[None, None])


def solution(mesh):
    placed = (
        P("section", ("groups", "pool"), None, None),
        P("section", ("groups", "pool"), None, None),
        P("section", ("groups", "pool"), None, None),
        P("section", None, None),
        P("section", None, None),
        P("section", None),
        P("section", None),
        P("section", ("groups", "pool"), None, None),
        P("section", ("groups", "pool"), None, None),
        P("section", ("groups", "pool"), None, None),
        P("section", ("groups", "pool"), None, None),
        P("section", ("groups", "pool"), None, None),
        P("section", ("groups", "pool")),
        P("section", ("groups", "pool"), None),
        P("section", ("groups", "pool")),
    )
    return jax.shard_map(
        on_device,
        mesh=mesh,
        in_specs=placed,
        out_specs=(
            P("section", ("groups", "pool"), None, None),
            P("section", ("groups", "pool"), None, None),
            P("section", ("groups", "pool"), None, None),
        ),
        check_vma=False,
    )
```
